128 devices in a mesh: pipe: 16 (over x, y), dp: 8 (over z, core).
Axes of the slice: x: 4, y: 4, z: 4, core: 2. Of those that a mesh axis runs over, the one named last changes fastest.
Arguments:
- stash_x: bfloat16 [16, 8, 12, 128, 4096], P('pipe', 'dp')
- stash_dy: bfloat16 [16, 8, 12, 128, 512], P('pipe', 'dp')
- queue: int32 [16, 12], P('pipe'), may hold values from 0 to 11, each once within a row
- micro_count: int32 [8], P('dp'), may hold values from 1 to 6, as said below
- master: float32 [16, 2, 4096, 512], P('pipe', None, 'dp'), may hold values from -6 to 6
- moment: float32 [16, 2, 4096, 512], P('pipe', None, 'dp'), may hold values from -0.3 to 0.3
- variance: float32 [16, 2, 4096, 512], P('pipe', None, 'dp'), may hold values from 0.0004 to 0.01
Outputs:
- new_master: float32 [16, 2, 4096, 512], P('pipe', None, 'dp')
- new_moment: float32 [16, 2, 4096, 512], P('pipe', None, 'dp')
- grad_norm: float32 [], replicated
The draws below stay inside these ranges and needn't reach their ends.
Inputs may be any that keep to these rules, and one draw needn't show every extreme that they name: `queue`: each row holds every code from 0 to 11 once. `micro_count`: in every draw some data replica has all 6 microbatches live.
All inputs are finite; a program needn't handle non-finite values.
Results may differ from the reference program's by a relative error of at most 0.002.
Values may be sent and summed in bfloat16 or wider, within the bound.
No kernel may reach another device: no remote copies, remote signals or barrier semaphores. Data moves between devices by JAX's collectives and lax.ppermute only.
A program may use at most 128 MiB of HBM per device.

```python
import math
import jax
import jax.numpy as jnp
from jax import lax

DIN = 4096
KVW = 512
MICRO = 6
MB_TOK = 128
SLOTS = 12
N_PIPE = 16
N_DP = 8


def draw_stash_x(key, part):
    key = jax.random.fold_in(key, 11)
    key_feature, key_main, key_common = jax.random.split(key, 3)
    feature = jnp.exp(jax.random.uniform(key_feature, (DIN,), jnp.float32, 0.0, math.log(10.0)))
    position = jnp.arange(DIN, dtype=jnp.float32) / max(DIN - 1, 1)
    shape = (N_PIPE, N_DP, SLOTS, MB_TOK, DIN)
    shared_shape = (N_PIPE, 1, SLOTS, MB_TOK, DIN)
    rising = 1.0 + 0.732 * position
    noise = jax.random.normal(key_main, shape, jnp.float32)
    common = jax.random.normal(key_common, shared_shape, jnp.float32)
    values = 0.6 * noise + 0.8 * common
    return (values * (feature * rising)).astype(jnp.bfloat16)


def draw_stash_dy(key, part):
    key = jax.random.fold_in(key, 23)
    key_column, key_main, key_common = jax.random.split(key, 3)
    column = jnp.exp(jax.random.uniform(key_column, (KVW,), jnp.float32, 0.0, math.log(10.0)))
    position = (jnp.arange(N_PIPE, dtype=jnp.float32) / max(N_PIPE - 1, 1)).reshape(N_PIPE, 1, 1, 1, 1)
    shape = (N_PIPE, N_DP, SLOTS, MB_TOK, KVW)
    shared_shape = (N_PIPE, 1, SLOTS, MB_TOK, KVW)
    rising = 1.0 + 0.732 * position
    noise = jax.random.normal(key_main, shape, jnp.float32)
    common = jax.random.normal(key_common, shared_shape, jnp.float32)
    values = 0.6 * noise + 0.8 * common
    return (values * column * rising).astype(jnp.bfloat16)


def draw_micro_count(key, part):
    key = jax.random.fold_in(key, 7)
    key_counts, key_full = jax.random.split(key)
    counts = jax.random.randint(key_counts, (N_DP,), 1, MICRO + 1, jnp.int32)
    full_rank = jax.random.randint(key_full, (), 0, N_DP, jnp.int32)
    return jnp.where(jnp.arange(N_DP, dtype=jnp.int32) == full_rank, MICRO, counts).astype(jnp.int32)


def level_of(own_key, extent, shards, low, largest):
    gain, own = 1.0, jax.random.fold_in(own_key, 6)
    for dim, blocks in shards:
        heights = jnp.exp(jax.random.uniform(jax.random.fold_in(own, dim), (blocks,), jnp.float32, low / len(shards), largest / len(shards)))
        gain = gain * jnp.repeat(heights, extent[dim] // blocks).reshape([-1 if axis == dim else 1 for axis in range(len(extent))])
    return gain


def gaussian(key, dims, deviation, bound, shards=(), kind=jnp.bfloat16):
    entries = deviation * jax.random.normal(key, dims, jnp.float32)
    if shards:
        entries = entries * level_of(key, dims, shards, -0.22, 0.18)
    return jnp.clip(entries, -bound, bound).astype(kind)


def setup_inputs(seed: int = 0) -> dict:
    keys = jax.random.split(jax.random.key(seed), 8)
    return {
        "stash_x": draw_stash_x(jax.random.fold_in(keys[7], 71), 0),
        "stash_dy": draw_stash_dy(jax.random.fold_in(keys[7], 71), 0),
        "queue": jax.vmap(lambda own: jax.random.permutation(own, SLOTS))(jax.random.split(keys[2], N_PIPE)).reshape((N_PIPE, SLOTS)).astype(jnp.int32),
        "micro_count": draw_micro_count(jax.random.fold_in(keys[7], 71), 0),
        "master": gaussian(keys[4], (N_PIPE, 2, DIN, KVW), 1.0, 6.0, ((0, 16), (2, 8)), jnp.float32),
        "moment": gaussian(keys[5], (N_PIPE, 2, DIN, KVW), 0.05, 0.3, ((0, 16), (2, 8)), jnp.float32),
        "variance": jnp.clip(jnp.exp(math.log(0.01) - 3.218876 * jax.random.uniform(keys[6], (N_PIPE, 2, DIN, KVW), jnp.float32) ** level_of(keys[6], (N_PIPE, 2, DIN, KVW), ((0, 16), (2, 8)), -0.2, 0.2)), 0.0004, 0.01),
    }


first_fix = 1.0 - 0.9 ** 20
second_fix = 1.0 - 0.95 ** 20

def section_slots(slot_order, virtual, micro_half):
    slot_codes = jnp.arange(micro_half, dtype=jnp.int32) + virtual * micro_half
    slot_total = slot_order.shape[0]
    matches = slot_order[None, :] == slot_codes[:, None]
    indices = jnp.arange(slot_total, dtype=jnp.int32)[None, :]
    return lax.optimization_barrier(jnp.sum(jnp.where(matches, indices, 0), axis=1)).astype(jnp.int32)

def reference(stash_x, stash_dy, queue, micro_count, master, moment, variance):
    slot_total = stash_x.shape[2]
    micro_half = slot_total // 2
    in_width = stash_x.shape[4]
    kv_width = stash_dy.shape[4]

    def pipe_grads(inputs):
        tokens_all, cotangent_all, slot_order = inputs

        def data_step(carry, data_inputs):
            tokens, cotangent, live_count = data_inputs
            sums = []
            for virtual in range(2):
                picked = section_slots(slot_order, virtual, micro_half)
                live_rows = (jnp.arange(micro_half, dtype=jnp.int32) < live_count).astype(cotangent.dtype)
                rows_x = jnp.take(tokens, picked, axis=0).reshape(-1, in_width)
                rows_y = (jnp.take(cotangent, picked, axis=0) * live_rows[:, None, None]).reshape(-1, kv_width)
                partial_sum = jnp.dot(rows_x.T, rows_y, preferred_element_type=jnp.float32).astype(jnp.bfloat16)
                partial_sum = lax.optimization_barrier(partial_sum)
                sums.append(partial_sum.astype(jnp.float32))
            return (carry + jnp.stack(sums), None)
        initial = jnp.zeros((2, in_width, kv_width), jnp.float32)
        summed, ignored = lax.scan(data_step, initial, (tokens_all, cotangent_all, micro_count))
        return summed
    gradient = lax.map(pipe_grads, (stash_x, stash_dy, queue))
    grad_norm = jnp.sqrt(jnp.sum(gradient * gradient))
    max_norm = 0.05 * jnp.sqrt(jnp.float32(gradient.size))
    clip_factor = jnp.minimum(jnp.float32(1.0), max_norm / (grad_norm + 1e-06))
    scaled = clip_factor * gradient
    new_moment = 0.9 * moment + 0.1 * scaled
    second = 0.95 * variance + 0.05 * scaled * scaled
    update = new_moment / first_fix / (jnp.sqrt(second / second_fix) + 1e-08)
    new_master = master - 0.01 * update - 0.001 * master
    return (new_master, new_moment, grad_norm)
```

```python
import functools
import math

import jax
import jax.numpy as jnp
from jax import lax
from jax.experimental import pallas as pl
from jax.experimental.pallas import tpu as pltpu
from jax.sharding import PartitionSpec as P

first_fix = 1.0 - 0.9**20
second_fix = 1.0 - 0.95**20

VMEM_LIMIT = 40 * 1024 * 1024


def place():
    me = lax.axis_index("dp")
    core = lax.rem(me, 2)
    return lax.div(me, 2), core, 1 - 2 * core


def section_kernel(step, mine, chips, *refs):
    queue, count, x_hbm, dy_hbm = refs[:4]
    others = refs[4:6] if mine else ()
    outs = refs[-6:-4]
    xbuf, ybuf, xsem, ysem = refs[-4:]
    slots, tokens, rows = xbuf.shape
    half = slots // 2
    z, core, sign = place()
    target = lax.rem(z + chips + step * sign, chips)
    owner = 2 * target + (core if mine else 1 - core)
    first = pl.multiple_of(owner * rows, rows)

    def copies(slot):
        code = queue[0, slot]
        return (
            pltpu.make_async_copy(x_hbm.at[0, 0, slot, :, pl.ds(first, rows)], xbuf.at[code], xsem.at[code]),
            pltpu.make_async_copy(dy_hbm.at[0, 0, slot], ybuf.at[code], ysem.at[code]),
        )

    for slot in range(slots):
        for copy in copies(slot):
            copy.start()
    live = count[0]
    width = ybuf.shape[2]
    tile = min(256, rows)
    for section in range(2):
        for code in range(section * half, (section + 1) * half):
            pltpu.make_async_copy(x_hbm.at[0, 0, 0, :, pl.ds(0, rows)], xbuf.at[code], xsem.at[code]).wait()
            pltpu.make_async_copy(dy_hbm.at[0, 0, 0], ybuf.at[code], ysem.at[code]).wait()
        span = slice(section * half, (section + 1) * half)
        dy = ybuf[span].reshape(half * tokens, width)
        micro = lax.broadcasted_iota(jnp.int32, (half * tokens, width), 0)
        dy = jnp.where(micro < live * tokens, dy, jnp.zeros_like(dy))
        for start in range(0, rows, tile):
            x = xbuf[span, :, start : start + tile].reshape(half * tokens, tile)
            total = lax.dot_general(x, dy, (((0,), (0,)), ((), ())), preferred_element_type=jnp.float32)
            if mine:
                total = total + others[section][start : start + tile, :].astype(jnp.float32)
            outs[section][start : start + tile, :] = total.astype(outs[section].dtype)


def section_rows(step, mine, chips, queue, count, x, dy, others=(), dtype=jnp.bfloat16):
    slots, tokens, features = x.shape[2:]
    width = dy.shape[4]
    rows = features // (2 * chips)
    smem = pl.BlockSpec(memory_space=pltpu.SMEM)
    hbm = pl.BlockSpec(memory_space=pl.ANY)
    vmem = pl.BlockSpec(memory_space=pltpu.VMEM)
    return pl.pallas_call(
        functools.partial(section_kernel, step, mine, chips),
        out_shape=(jax.ShapeDtypeStruct((rows, width), dtype),) * 2,
        in_specs=[smem, smem, hbm, hbm] + [vmem] * len(others),
        out_specs=(vmem, vmem),
        scratch_shapes=[
            pltpu.VMEM((slots, tokens, rows), x.dtype),
            pltpu.VMEM((slots, tokens, width), dy.dtype),
            pltpu.SemaphoreType.DMA((slots,)),
            pltpu.SemaphoreType.DMA((slots,)),
        ],
        compiler_params=pltpu.CompilerParams(vmem_limit_bytes=VMEM_LIMIT),
        cost_estimate=pl.CostEstimate(
            flops=2 * slots * tokens * rows * width,
            bytes_accessed=2 * slots * tokens * (rows + width) + 4 * rows * width,
            transcendentals=0,
        ),
        name=f"section_rows_{'keep' if mine else 'send'}_{step}",
    )(queue, count, x, dy, *others)


def sum_kernel(a, b, out):
    out[...] = (a[...].astype(jnp.float32) + b[...].astype(jnp.float32)).astype(out.dtype)


def add(a, b):
    return pl.pallas_call(sum_kernel, out_shape=jax.ShapeDtypeStruct(a.shape, a.dtype), name="ring_add")(a, b)


def total_kernel(own0, own1, a0, b0, a1, b1, grad, squares):
    norm = jnp.zeros((), jnp.float32)
    for section, parts in enumerate(((own0, a0, b0), (own1, a1, b1))):
        total = sum(part[...].astype(jnp.float32) for part in parts)
        grad[section] = total
        norm = norm + jnp.sum(total * total)
    squares[...] = jnp.full(squares.shape, norm, jnp.float32)


def totals(peers, own, a0, b0, a1, b1):
    rows, width = own[0].shape
    return pl.pallas_call(
        total_kernel,
        out_shape=(
            jax.ShapeDtypeStruct((2, rows, width), jnp.float32),
            jax.ShapeDtypeStruct((peers, 128), jnp.float32),
        ),
        compiler_params=pltpu.CompilerParams(vmem_limit_bytes=VMEM_LIMIT),
        name="totals",
    )(*own, a0, b0, a1, b1)


def update_kernel(max_norm, squares, grad, master, moment, variance, new_master, new_moment, norm_out):
    norm = jnp.sqrt(jnp.sum(squares[:, 0:1]))
    clip = jnp.minimum(jnp.float32(1.0), max_norm / (norm + 1e-06))
    norm_out[0, 0] = norm
    scaled = clip * grad[...]
    fresh = 0.9 * moment[...] + 0.1 * scaled
    second = 0.95 * variance[...] + 0.05 * scaled * scaled
    update = fresh / first_fix / (jnp.sqrt(second / second_fix) + 1e-08)
    new_moment[...] = fresh
    new_master[...] = master[...] - 0.01 * update - 0.001 * master[...]


def adam(max_norm, squares, grad, master, moment, variance):
    sections, rows, width = grad.shape
    tile = 128
    block = pl.BlockSpec((1, tile, width), lambda s, i: (s, i, 0))
    state = jax.ShapeDtypeStruct(grad.shape, jnp.float32)
    return pl.pallas_call(
        functools.partial(update_kernel, max_norm),
        grid=(sections, rows // tile),
        out_shape=(state, state, jax.ShapeDtypeStruct((1, 1), jnp.float32)),
        in_specs=[pl.BlockSpec(memory_space=pltpu.VMEM), block, block, block, block],
        out_specs=(block, block, pl.BlockSpec(memory_space=pltpu.SMEM)),
        compiler_params=pltpu.CompilerParams(vmem_limit_bytes=VMEM_LIMIT),
        name="adam",
    )(squares, grad, master, moment, variance)


def on_device(stash_x, stash_dy, queue, micro_count, master, moment, variance):
    own_rows, kv_width = master.shape[2:]
    peers = lax.axis_size("dp")
    chips = peers // 2
    everyone = lax.axis_size("pipe") * peers

    def ring(sign):
        return [
            (i, (i // 2 + sign * (1 - 2 * (i % 2))) % chips * 2 + i % 2) for i in range(peers)
        ]

    def sibling(value):
        return lax.ppermute(value, "dp", [(i, i ^ 1) for i in range(peers)])

    def along(value):
        return lax.ppermute(value, "dp", ring(1))

    def against(value):
        return lax.ppermute(value, "dp", ring(-1))

    rows = functools.partial(section_rows, chips=chips, queue=queue, count=micro_count, x=stash_x, dy=stash_dy)

    def chip_rows(step, dtype=jnp.bfloat16):
        sent = rows(-step, False)
        return rows(step, True, others=tuple(sibling(value) for value in sent), dtype=dtype)

    far = chip_rows(2)
    far_a, far_b = along(far[0]), against(far[1])
    near_a = chip_rows(1)
    near_b = chip_rows(-1)
    plain_a = along(near_a[1])
    plain_b = against(near_b[0])
    own = chip_rows(0, jnp.float32)
    sum_a = along(add(near_a[0], far_a))
    sum_b = against(add(near_b[1], far_b))
    grad, squares = totals(everyone, own, sum_a, plain_b, plain_a, sum_b)
    squares = lax.all_to_all(squares, ("pipe", "dp"), 0, 0, tiled=True)
    max_norm = 0.05 * math.sqrt(2 * lax.axis_size("pipe") * own_rows * peers * kv_width)
    new_master, new_moment, norm = adam(max_norm, squares, grad, master[0], moment[0], variance[0])
    return (new_master[None], new_moment[None], norm[0, 0])


def solution(mesh):
    in_specs = (
        P("pipe", "dp", None, None, None),
        P("pipe", "dp", None, None, None),
        P("pipe", None),
        P("dp"),
        P("pipe", None, "dp", None),
        P("pipe", None, "dp", None),
        P("pipe", None, "dp", None),
    )
    out_specs = (P("pipe", None, "dp", None), P("pipe", None, "dp", None), P())
    return jax.shard_map(
        on_device, mesh=mesh, in_specs=in_specs, out_specs=out_specs, check_vma=False
    )
```

```python
import functools
import math

import jax
import jax.numpy as jnp
from jax import lax
from jax.experimental import pallas as pl
from jax.experimental.pallas import tpu as pltpu
from jax.sharding import PartitionSpec as P

first_fix = 1.0 - 0.9**20
second_fix = 1.0 - 0.95**20

def vmem_limit(mib):
    return pltpu.CompilerParams(vmem_limit_bytes=mib * 1024 * 1024)


def place():
    me = lax.axis_index("dp")
    core = lax.rem(me, 2)
    return lax.div(me, 2), core, 1 - 2 * core


def owner_of(block, chips):
    step, mine = block
    z, core, sign = place()
    target = lax.rem(z + chips + step * sign, chips)
    return 2 * target + (core if mine else 1 - core)


def section_product(section, queue, count, x_of, rows, dy_ref, tile, store):
    slots = dy_ref.shape[0]
    width = dy_ref.shape[2]
    half = slots // 2
    live = count[0]
    picked = []
    for micro in range(half):
        slot = jnp.int32(0)
        for place_in_stash in range(slots):
            slot = jnp.where(queue[0, place_in_stash] == section * half + micro, place_in_stash, slot)
        picked.append(slot)
    dy = []
    for micro, slot in enumerate(picked):
        value = dy_ref[slot]
        dy.append(jnp.where(micro < live, value, jnp.zeros_like(value)))
    dy = jnp.concatenate(dy, axis=0)
    for start in range(0, rows, tile):
        x = jnp.concatenate([x_of(slot, start, tile) for slot in picked], axis=0)
        store(
            start,
            lax.dot_general(x, dy, (((0,), (0,)), ((), ())), preferred_element_type=jnp.float32),
        )


def product_kernel(sections, chips, block, n_others, n_ready, stacked, *refs):
    queue, count, x_ref, dy_ref = refs[:4]
    others = refs[4 : 4 + n_others]
    ready = refs[4 + n_others : 4 + n_others + n_ready]
    outs = refs[4 + n_others + n_ready :]
    rows = outs[0].shape[-2]
    tile = min(256, rows)
    first = owner_of(block, chips) * rows

    def x_of(slot, start, size):
        if len(x_ref.shape) == 3:
            return x_ref[slot, :, start : start + size]
        return x_ref[0, 0, slot, :, pl.ds(pl.multiple_of(first + start, size), size)]

    for i, value in enumerate(ready):
        outs[0][i] = value[...]
    for i, section in enumerate(sections):

        def store(start, total, i=i):
            span = pl.ds(start, tile)
            if others:
                other = others[i][span, :] if len(others) == len(sections) else others[0][i, span, :]
                total = total + other.astype(jnp.float32)
            if stacked:
                outs[0][n_ready + i, span, :] = total.astype(outs[0].dtype)
            else:
                outs[i][span, :] = total.astype(outs[i].dtype)

        section_product(section, queue, count, x_of, rows, dy_ref, tile, store)


def first_kernel(chips, blocks, queue_hbm, count, x_hbm, dy_hbm, out, dy_ref, *rest):
    buffers, (queue, sems) = rest[:-2], rest[-2:]
    rows = buffers[0].shape[2]
    copies = [
        pltpu.make_async_copy(queue_hbm, queue, sems.at[0]),
        pltpu.make_async_copy(dy_hbm.at[0, 0], dy_ref, sems.at[1]),
    ]
    for i, (block, buffer) in enumerate(zip(blocks, buffers)):
        first = pl.multiple_of(owner_of(block, chips) * rows, rows)
        copies.append(pltpu.make_async_copy(x_hbm.at[0, 0, :, :, pl.ds(first, rows)], buffer, sems.at[2 + i]))
    for copy in copies:
        copy.start()
    for copy in copies[:3]:
        copy.wait()
    tile = min(256, rows)

    def x_of(slot, start, size):
        return buffers[0][slot, :, start : start + size]

    def store(start, total):
        out[pl.ds(start, tile), :] = total.astype(out.dtype)

    section_product(0, queue, count, x_of, rows, dy_ref, tile, store)
    for copy in copies[3:]:
        copy.wait()


COSTS = dict()


def cost(name):
    return pl.CostEstimate(flops=COSTS.get(name, 1), bytes_accessed=1, transcendentals=0)


SMEM = pl.BlockSpec(memory_space=pltpu.SMEM)
VMEM = pl.BlockSpec(memory_space=pltpu.VMEM)
HBM = pl.BlockSpec(memory_space=pl.ANY)


def first_product(queue, count, x, dy, chips, blocks):
    slots, tokens, features = x.shape[2:]
    width = dy.shape[4]
    rows = features // (2 * chips)
    return pl.pallas_call(
        functools.partial(first_kernel, chips, blocks),
        out_shape=(
            jax.ShapeDtypeStruct((rows, width), jnp.bfloat16),
            jax.ShapeDtypeStruct((slots, tokens, width), dy.dtype),
        )
        + (jax.ShapeDtypeStruct((slots, tokens, rows), x.dtype),) * len(blocks),
        in_specs=[HBM, SMEM, HBM, HBM],
        out_specs=(VMEM,) * (2 + len(blocks)),
        scratch_shapes=[
            pltpu.SMEM(queue.shape, queue.dtype),
            pltpu.SemaphoreType.DMA((2 + len(blocks),)),
        ],
        compiler_params=vmem_limit(12),
        cost_estimate=cost("first_product"),
        name="first_product",
    )(queue, count, x, dy)


def product(queue, count, x, dy, block, chips, rows, sections=(0, 1), others=(), ready=(), stacked=False, dtype=jnp.bfloat16, name=""):
    width = dy.shape[2]
    if stacked:
        outs = (jax.ShapeDtypeStruct((len(ready) + len(sections), rows, width), dtype),)
    else:
        outs = (jax.ShapeDtypeStruct((rows, width), dtype),) * len(sections)
    return pl.pallas_call(
        functools.partial(product_kernel, sections, chips, block, len(others), len(ready), stacked),
        out_shape=outs,
        in_specs=[SMEM, SMEM] + [VMEM] * (2 + len(others) + len(ready)),
        out_specs=(VMEM,) * len(outs),
        compiler_params=vmem_limit(8),
        cost_estimate=cost(name),
        name=name,
    )(queue, count, x, dy, *others, *ready)


def sum_kernel(a, b, out):
    sections, rows, _ = a.shape
    slab = 64
    per = rows // slab

    def step(i, carry):
        section, span = lax.div(i, per), pl.ds(pl.multiple_of(lax.rem(i, per) * slab, slab), slab)
        out[section, span, :] = (
            a[section, span, :].astype(jnp.float32) + b[section, span, :].astype(jnp.float32)
        ).astype(out.dtype)
        return carry

    lax.fori_loop(0, sections * per, step, 0)


def add(a, b):
    return pl.pallas_call(
        sum_kernel,
        out_shape=jax.ShapeDtypeStruct(a.shape, a.dtype),
        in_specs=[VMEM, VMEM],
        out_specs=VMEM,
        compiler_params=vmem_limit(4),
        cost_estimate=cost("ring_add"),
        name="ring_add",
    )(a, b)


def total_kernel(own, summed, plain, grad, squares):
    slab = 16
    _, rows, width = own.shape

    def step(i, kept):
        span = pl.ds(pl.multiple_of(i * slab, slab), slab)
        for section in range(own.shape[0]):
            total = own[section, span, :] + summed[section, span, :].astype(jnp.float32)
            total = total + plain[section, span, :].astype(jnp.float32)
            grad[section, span, :] = total
            kept = kept + total * total
        return kept

    kept = lax.fori_loop(0, rows // slab, step, jnp.zeros((slab, width), jnp.float32))
    squares[...] = jnp.full(squares.shape, jnp.sum(kept), jnp.float32)


def totals(peers, own, summed, plain):
    return pl.pallas_call(
        total_kernel,
        out_shape=(
            jax.ShapeDtypeStruct(own.shape, jnp.float32),
            jax.ShapeDtypeStruct((peers, 128), jnp.float32),
        ),
        in_specs=[VMEM] * 3,
        out_specs=(VMEM, VMEM),
        compiler_params=vmem_limit(4),
        cost_estimate=cost("totals"),
        name="totals",
    )(own, summed, plain)


def update_kernel(max_norm, squares, grad, master, moment, variance, new_master, new_moment, norm_out, masters, moments, sems):
    norm = jnp.sqrt(jnp.sum(squares[:, 0:1]))
    clip = jnp.minimum(jnp.float32(1.0), max_norm / (norm + 1e-06))
    norm_out[0, 0] = norm
    sections, rows, width = grad.shape
    chunk, slab = 128, 64
    per = rows // chunk

    def copies(i):
        section, span = lax.div(i, per), pl.ds(pl.multiple_of(lax.rem(i, per) * chunk, chunk), chunk)
        return (
            pltpu.make_async_copy(masters.at[section, span], new_master.at[section, span], sems.at[0, i]),
            pltpu.make_async_copy(moments.at[section, span], new_moment.at[section, span], sems.at[1, i]),
        )

    def one(i, carry):
        section = lax.div(i, per)

        def step(j, inner):
            span = pl.ds(pl.multiple_of(lax.rem(i, per) * chunk + j * slab, slab), slab)
            scaled = clip * grad[section, span, :]
            fresh = 0.9 * moment[section, span, :] + 0.1 * scaled
            second = (0.95 / second_fix) * variance[section, span, :] + (0.05 / second_fix) * (scaled * scaled)
            update = ((0.01 / first_fix) * fresh) / (jnp.sqrt(second) + 1e-08)
            moments[section, span, :] = fresh
            masters[section, span, :] = (1.0 - 0.001) * master[section, span, :] - update
            return inner

        lax.fori_loop(0, chunk // slab, step, 0)
        for copy in copies(i):
            copy.start()
        return carry

    lax.fori_loop(0, sections * per, one, 0)

    def finish(i, carry):
        for copy in copies(i):
            copy.wait()
        return carry

    lax.fori_loop(0, sections * per, finish, 0)


def adam(max_norm, squares, grad, master, moment, variance):
    sections, rows, width = grad.shape
    state = jax.ShapeDtypeStruct(grad.shape, jnp.float32)
    return pl.pallas_call(
        functools.partial(update_kernel, max_norm),
        out_shape=(state, state, jax.ShapeDtypeStruct((1, 1), jnp.float32)),
        in_specs=[VMEM] * 5,
        out_specs=(HBM, HBM, SMEM),
        scratch_shapes=[
            pltpu.VMEM(grad.shape, jnp.float32),
            pltpu.VMEM(grad.shape, jnp.float32),
            pltpu.SemaphoreType.DMA((2, sections * rows // 128)),
        ],
        compiler_params=vmem_limit(8),
        cost_estimate=cost("adam"),
        name="adam",
    )(squares, grad, master, moment, variance)


def after(value, *earlier):
    return lax.optimization_barrier((value, earlier))[0]


def on_device(stash_x, stash_dy, queue, micro_count, master, moment, variance):
    own_rows, kv_width = master.shape[2:]
    peers = lax.axis_size("dp")
    chips = peers // 2
    everyone = lax.axis_size("pipe") * peers
    hbm_queue, hbm_x, hbm_dy = (
        pltpu.with_memory_space_constraint(value, pltpu.HBM) for value in (queue, stash_x, stash_dy)
    )

    def ring(sign):
        return [
            (i, (i // 2 + sign * (1 - 2 * (i % 2))) % chips * 2 + i % 2) for i in range(peers)
        ]

    def sibling(value):
        return lax.ppermute(value, "dp", [(i, i ^ 1) for i in range(peers)])

    def along(value):
        return lax.ppermute(value, "dp", ring(1))

    def against(value):
        return lax.ppermute(value, "dp", ring(-1))

    sent_a, dy, x_send, x_keep = first_product(hbm_queue, micro_count, hbm_x, hbm_dy, chips, ((-2, False), (2, True)))
    other_a = sibling(sent_a)
    block = functools.partial(product, queue, micro_count, chips=chips, rows=own_rows)
    (sent_b,) = block(x_send, dy, (-2, False), sections=(1,), name="far_send_b")
    other_b = sibling(sent_b)
    others = {}

    def send(step, dy):
        sent = block(stash_x, dy, (step, False), name=f"send_{step % chips}")
        others[-step] = [sibling(value) for value in sent]
        return sent[0]

    def keep(step, dy, dtype=jnp.bfloat16):
        (kept,) = block(stash_x, dy, (step, True), others=others[step], stacked=True, dtype=dtype, name=f"keep_{step % chips}")
        return kept

    (far_a,) = block(x_keep, after(dy, sent_b), (2, True), sections=(0,), others=(other_a,), name="far_keep_a")
    (far,) = block(
        x_keep, after(dy, far_a), (2, True), sections=(1,), others=(other_b,), ready=(far_a,), stacked=True, name="far_keep_b"
    )
    came = along(far)
    dy = after(dy, send(1, after(dy, far)))
    dy = after(dy, send(-1, dy))
    near_b = keep(-1, dy)
    plain = against(near_b)
    near_a = keep(1, after(dy, near_b))
    near_a = add(near_a, came)
    summed = along(near_a)
    dy = after(dy, send(0, after(dy, near_a)))
    own = keep(0, dy, jnp.float32)
    grad, squares = totals(everyone, own, summed, plain)
    squares = lax.all_to_all(squares, ("pipe", "dp"), 0, 0, tiled=True)
    max_norm = 0.05 * math.sqrt(2 * lax.axis_size("pipe") * own_rows * peers * kv_width)
    new_master, new_moment, norm = adam(max_norm, squares, grad, master[0], moment[0], variance[0])
    return (new_master[None], new_moment[None], norm[0, 0])


def solution(mesh):
    in_specs = (
        P("pipe", "dp", None, None, None),
        P("pipe", "dp", None, None, None),
        P("pipe", None),
        P("dp"),
        P("pipe", None, "dp", None),
        P("pipe", None, "dp", None),
        P("pipe", None, "dp", None),
    )
    out_specs = (P("pipe", None, "dp", None), P("pipe", None, "dp", None), P())
    return jax.shard_map(
        on_device, mesh=mesh, in_specs=in_specs, out_specs=out_specs, check_vma=False
    )
```

```python
import functools
import math

import jax
import jax.numpy as jnp
from jax import lax
from jax.experimental import pallas as pl
from jax.experimental.pallas import tpu as pltpu
from jax.sharding import PartitionSpec as P

first_fix = 1.0 - 0.9**20
second_fix = 1.0 - 0.95**20

def vmem_limit(mib):
    return pltpu.CompilerParams(vmem_limit_bytes=mib * 1024 * 1024)


def place():
    me = lax.axis_index("dp")
    core = lax.rem(me, 2)
    return lax.div(me, 2), core, 1 - 2 * core


def owner_of(block, chips):
    step, mine = block
    z, core, sign = place()
    target = lax.rem(z + chips + step * sign, chips)
    return 2 * target + (core if mine else 1 - core)


def section_product(slots, section, x_of, dy_ref, rows, store):
    tile = min(256, rows)
    for start in range(0, rows, tile):
        x = jnp.concatenate([x_of(slot, start, tile) for slot in slots], axis=0)
        store(
            pl.ds(start, tile),
            lax.dot_general(x, dy_ref[section], (((0,), (0,)), ((), ())), preferred_element_type=jnp.float32),
        )


def product_kernel(section, chips, block, has_other, place_in, *refs):
    plan, x_ref, dy_ref = refs[:3]
    out = refs[-1]
    rows = out.shape[-2]
    half = plan.shape[0] // 2
    slots = [plan[section * half + micro, 0] for micro in range(half)]
    first = owner_of(block, chips) * rows

    def x_of(slot, start, size):
        if len(x_ref.shape) == 3:
            return x_ref[slot, :, start : start + size]
        return x_ref[0, 0, slot, :, pl.ds(pl.multiple_of(first + start, size), size)]

    def store(span, total):
        if has_other:
            total = total + refs[3][span, :].astype(jnp.float32)
        if place_in is None:
            out[span, :] = total.astype(out.dtype)
        else:
            out[place_in, span, :] = total.astype(out.dtype)

    section_product(slots, section, x_of, dy_ref, rows, store)


def first_kernel(chips, blocks, queue_hbm, count, x_hbm, dy_hbm, out, plan, dy_ref, *rest):
    buffers, (raw, queue, slot_of, sems) = rest[:-4], rest[-4:]
    rows = buffers[0].shape[2]
    slots, tokens, _ = raw.shape
    half = slots // 2
    copies = [
        pltpu.make_async_copy(queue_hbm, queue, sems.at[0]),
        pltpu.make_async_copy(dy_hbm.at[0, 0], raw, sems.at[1]),
    ]
    for i, (block, buffer) in enumerate(zip(blocks, buffers)):
        first = pl.multiple_of(owner_of(block, chips) * rows, rows)
        copies.append(pltpu.make_async_copy(x_hbm.at[0, 0, :, :, pl.ds(first, rows)], buffer, sems.at[2 + i]))
    for copy in copies:
        copy.start()
    copies[0].wait()
    for slot in range(slots):
        code = queue[0, slot]
        slot_of[code] = slot
        plan[pl.ds(code, 1), :] = jnp.full((1, plan.shape[1]), slot, jnp.int32)
    live = count[0]

    def order_dy(section):
        for micro in range(half):
            value = raw[slot_of[section * half + micro]]
            dy_ref[section, micro * tokens : (micro + 1) * tokens, :] = jnp.where(
                micro < live, value, jnp.zeros_like(value)
            )

    copies[1].wait()
    order_dy(0)
    copies[2].wait()

    def x_of(slot, start, size):
        return buffers[0][slot, :, start : start + size]

    def store(span, total):
        out[span, :] = total.astype(out.dtype)

    section_product([slot_of[micro] for micro in range(half)], 0, x_of, dy_ref, rows, store)
    order_dy(1)
    for copy in copies[3:]:
        copy.wait()


COSTS = dict()


def cost(name):
    return pl.CostEstimate(flops=COSTS.get(name, 1), bytes_accessed=1, transcendentals=0)


SMEM = pl.BlockSpec(memory_space=pltpu.SMEM)
VMEM = pl.BlockSpec(memory_space=pltpu.VMEM)
HBM = pl.BlockSpec(memory_space=pl.ANY)


def first_product(queue, count, x, dy, chips, blocks):
    slots, tokens, features = x.shape[2:]
    width = dy.shape[4]
    rows = features // (2 * chips)
    return pl.pallas_call(
        functools.partial(first_kernel, chips, blocks),
        out_shape=(
            jax.ShapeDtypeStruct((rows, width), jnp.bfloat16),
            jax.ShapeDtypeStruct((slots, 128), jnp.int32),
            jax.ShapeDtypeStruct((2, slots // 2 * tokens, width), dy.dtype),
        )
        + (jax.ShapeDtypeStruct((slots, tokens, rows), x.dtype),) * len(blocks),
        in_specs=[HBM, SMEM, HBM, HBM],
        out_specs=(VMEM,) * (3 + len(blocks)),
        scratch_shapes=[
            pltpu.VMEM((slots, tokens, width), dy.dtype),
            pltpu.SMEM(queue.shape, queue.dtype),
            pltpu.SMEM((slots,), jnp.int32),
            pltpu.SemaphoreType.DMA((2 + len(blocks),)),
        ],
        compiler_params=vmem_limit(12),
        cost_estimate=cost("first_product"),
        name="first_product",
    )(queue, count, x, dy)


def product(plan, x, dy, block, section, chips, rows, other=None, stacked=False, beside=None, dtype=jnp.bfloat16, name=""):
    width = dy.shape[2]
    operands = [plan, x, dy] + ([] if other is None else [other]) + ([] if beside is None else [beside])
    shape = (2, rows, width) if stacked else (rows, width)
    return pl.pallas_call(
        functools.partial(product_kernel, section, chips, block, other is not None, section if stacked else None),
        out_shape=jax.ShapeDtypeStruct(shape, dtype),
        in_specs=[VMEM] * len(operands),
        out_specs=VMEM,
        input_output_aliases={} if beside is None else {len(operands) - 1: 0},
        compiler_params=vmem_limit(8),
        cost_estimate=cost(name),
        name=name,
    )(*operands)


def sum_kernel(a, b, out):
    sections, rows, _ = a.shape
    slab = 64
    per = rows // slab

    def step(i, carry):
        section, span = lax.div(i, per), pl.ds(pl.multiple_of(lax.rem(i, per) * slab, slab), slab)
        out[section, span, :] = (
            a[section, span, :].astype(jnp.float32) + b[section, span, :].astype(jnp.float32)
        ).astype(out.dtype)
        return carry

    lax.fori_loop(0, sections * per, step, 0)


def add(a, b):
    return pl.pallas_call(
        sum_kernel,
        out_shape=jax.ShapeDtypeStruct(a.shape, a.dtype),
        in_specs=[VMEM, VMEM],
        out_specs=VMEM,
        compiler_params=vmem_limit(4),
        cost_estimate=cost("ring_add"),
        name="ring_add",
    )(a, b)


def total_kernel(own, summed, plain, grad, squares):
    slab = 16
    _, rows, width = own.shape

    def step(i, kept):
        span = pl.ds(pl.multiple_of(i * slab, slab), slab)
        for section in range(own.shape[0]):
            total = own[section, span, :] + summed[section, span, :].astype(jnp.float32)
            total = total + plain[section, span, :].astype(jnp.float32)
            grad[section, span, :] = total
            kept = kept + total * total
        return kept

    kept = lax.fori_loop(0, rows // slab, step, jnp.zeros((slab, width), jnp.float32))
    squares[...] = jnp.full(squares.shape, jnp.sum(kept), jnp.float32)


def totals(peers, own, summed, plain):
    return pl.pallas_call(
        total_kernel,
        out_shape=(
            jax.ShapeDtypeStruct(own.shape, jnp.float32),
            jax.ShapeDtypeStruct((peers, 128), jnp.float32),
        ),
        in_specs=[VMEM] * 3,
        out_specs=(VMEM, VMEM),
        compiler_params=vmem_limit(4),
        cost_estimate=cost("totals"),
        name="totals",
    )(own, summed, plain)


def update_kernel(max_norm, squares, grad, master, moment, variance, new_master, new_moment, norm_out, masters, moments, sems):
    norm = jnp.sqrt(jnp.sum(squares[:, 0:1]))
    clip = jnp.minimum(jnp.float32(1.0), max_norm / (norm + 1e-06))
    norm_out[0, 0] = norm
    sections, rows, width = grad.shape
    chunk, slab = 128, 64
    per = rows // chunk

    def copies(i):
        section, span = lax.div(i, per), pl.ds(pl.multiple_of(lax.rem(i, per) * chunk, chunk), chunk)
        return (
            pltpu.make_async_copy(masters.at[section, span], new_master.at[section, span], sems.at[0, i]),
            pltpu.make_async_copy(moments.at[section, span], new_moment.at[section, span], sems.at[1, i]),
        )

    def one(i, carry):
        section = lax.div(i, per)

        def step(j, inner):
            span = pl.ds(pl.multiple_of(lax.rem(i, per) * chunk + j * slab, slab), slab)
            scaled = clip * grad[section, span, :]
            fresh = 0.9 * moment[section, span, :] + 0.1 * scaled
            second = (0.95 / second_fix) * variance[section, span, :] + (0.05 / second_fix) * (scaled * scaled)
            update = ((0.01 / first_fix) * fresh) / (second * lax.rsqrt(second) + 1e-08)
            moments[section, span, :] = fresh
            masters[section, span, :] = (1.0 - 0.001) * master[section, span, :] - update
            return inner

        lax.fori_loop(0, chunk // slab, step, 0)
        for copy in copies(i):
            copy.start()
        return carry

    lax.fori_loop(0, sections * per, one, 0)

    def finish(i, carry):
        for copy in copies(i):
            copy.wait()
        return carry

    lax.fori_loop(0, sections * per, finish, 0)


def adam(max_norm, squares, grad, master, moment, variance):
    sections, rows, width = grad.shape
    state = jax.ShapeDtypeStruct(grad.shape, jnp.float32)
    return pl.pallas_call(
        functools.partial(update_kernel, max_norm),
        out_shape=(state, state, jax.ShapeDtypeStruct((1, 1), jnp.float32)),
        in_specs=[VMEM] * 5,
        out_specs=(HBM, HBM, SMEM),
        scratch_shapes=[
            pltpu.VMEM(grad.shape, jnp.float32),
            pltpu.VMEM(grad.shape, jnp.float32),
            pltpu.SemaphoreType.DMA((2, sections * rows // 128)),
        ],
        compiler_params=vmem_limit(8),
        cost_estimate=cost("adam"),
        name="adam",
    )(squares, grad, master, moment, variance)


def after(value, *earlier):
    return lax.optimization_barrier((value, earlier))[0]


def on_device(stash_x, stash_dy, queue, micro_count, master, moment, variance):
    own_rows, kv_width = master.shape[2:]
    peers = lax.axis_size("dp")
    chips = peers // 2
    everyone = lax.axis_size("pipe") * peers
    hbm_queue, hbm_x, hbm_dy = (
        pltpu.with_memory_space_constraint(value, pltpu.HBM) for value in (queue, stash_x, stash_dy)
    )

    held_x = pltpu.with_memory_space_constraint(stash_x, pltpu.VMEM)

    def ring(sign):
        return [
            (i, (i // 2 + sign * (1 - 2 * (i % 2))) % chips * 2 + i % 2) for i in range(peers)
        ]

    def sibling(value):
        return lax.ppermute(value, "dp", [(i, i ^ 1) for i in range(peers)])

    def along(value):
        return lax.ppermute(value, "dp", ring(1))

    def against(value):
        return lax.ppermute(value, "dp", ring(-1))

    sent_a, plan, dy, x_send, x_keep = first_product(hbm_queue, micro_count, hbm_x, hbm_dy, chips, ((-2, False), (2, True)))
    far_other = [sibling(sent_a)]
    block = functools.partial(product, plan, chips=chips, rows=own_rows)
    sent_b = block(x_send, dy, (-2, False), 1, name="far_send_b")
    far_other.append(sibling(sent_b))
    others = {}

    def send(step, dy):
        others[-step] = []
        for section in range(2):
            sent = block(held_x, dy, (step, False), section, name=f"send_{step % chips}{'ab'[section]}")
            others[-step].append(sibling(sent))
            dy = after(dy, sent)
        return dy

    def keep(step, x, other, dy, dtype=jnp.bfloat16):
        kept = None
        for section in range(2):
            kept = block(
                x,
                dy,
                (step, True),
                section,
                other=other[section],
                stacked=True,
                beside=kept,
                dtype=dtype,
                name=f"keep_{step % chips}{'ab'[section]}",
            )
            dy = after(dy, kept)
        return kept

    far = keep(2, x_keep, far_other, after(dy, sent_b))
    came = along(far)
    dy = send(-1, after(dy, far))
    dy = send(1, dy)
    near_a = keep(1, held_x, others[1], dy)
    near_b = keep(-1, held_x, others[-1], after(dy, near_a))
    plain = against(near_b)
    near_a = add(after(near_a, near_b), came)
    summed = along(near_a)
    dy = send(0, after(dy, near_a))
    own = keep(0, held_x, others[0], dy, jnp.float32)
    grad, squares = totals(everyone, own, summed, plain)
    squares = lax.all_to_all(squares, ("pipe", "dp"), 0, 0, tiled=True)
    max_norm = 0.05 * math.sqrt(2 * lax.axis_size("pipe") * own_rows * peers * kv_width)
    new_master, new_moment, norm = adam(max_norm, squares, grad, master[0], moment[0], variance[0])
    return (new_master[None], new_moment[None], norm[0, 0])


def solution(mesh):
    in_specs = (
        P("pipe", "dp", None, None, None),
        P("pipe", "dp", None, None, None),
        P("pipe", None),
        P("dp"),
        P("pipe", None, "dp", None),
        P("pipe", None, "dp", None),
        P("pipe", None, "dp", None),
    )
    out_specs = (P("pipe", None, "dp", None), P("pipe", None, "dp", None), P())
    return jax.shard_map(
        on_device, mesh=mesh, in_specs=in_specs, out_specs=out_specs, check_vma=False
    )
```

```python
import functools
import math

import jax
import jax.numpy as jnp
from jax import lax
from jax.experimental import pallas as pl
from jax.experimental.pallas import tpu as pltpu
from jax.sharding import PartitionSpec as P

first_fix = 1.0 - 0.9**20
second_fix = 1.0 - 0.95**20

def vmem_limit(mib):
    return pltpu.CompilerParams(vmem_limit_bytes=mib * 1024 * 1024)


def place():
    me = lax.axis_index("dp")
    core = lax.rem(me, 2)
    return lax.div(me, 2), core, 1 - 2 * core


def owner_of(block, chips):
    step, mine = block
    z, core, sign = place()
    target = lax.rem(z + chips + step * sign, chips)
    return 2 * target + (core if mine else 1 - core)


def section_product(slots, section, x_of, dy_ref, rows, store):
    tile = min(256, rows)
    for start in range(0, rows, tile):
        x = jnp.concatenate([x_of(slot, start, tile) for slot in slots], axis=0)
        store(
            pl.ds(start, tile),
            lax.dot_general(x, dy_ref[section], (((0,), (0,)), ((), ())), preferred_element_type=jnp.float32),
        )


def product_kernel(section, chips, block, has_other, place_in, *refs):
    plan, x_ref, dy_ref = refs[:3]
    out = refs[-1]
    rows = out.shape[-2]
    half = plan.shape[0] // 2
    slots = [plan[section * half + micro, 0] for micro in range(half)]
    first = owner_of(block, chips) * rows

    def x_of(slot, start, size):
        if len(x_ref.shape) == 3:
            return x_ref[slot, :, start : start + size]
        return x_ref[0, 0, slot, :, pl.ds(pl.multiple_of(first + start, size), size)]

    def store(span, total):
        if has_other:
            total = total + refs[3][span, :].astype(jnp.float32)
        if place_in is None:
            out[span, :] = total.astype(out.dtype)
        else:
            out[place_in, span, :] = total.astype(out.dtype)

    section_product(slots, section, x_of, dy_ref, rows, store)


def first_kernel(chips, blocks, queue_hbm, count, x_hbm, dy_hbm, out, plan, dy_ref, *rest):
    buffers, (raw, queue, slot_of, sems) = rest[:-4], rest[-4:]
    rows = buffers[0].shape[2]
    slots, tokens, _ = raw.shape
    half = slots // 2
    copies = [
        pltpu.make_async_copy(queue_hbm, queue, sems.at[0]),
        pltpu.make_async_copy(dy_hbm.at[0, 0], raw, sems.at[1]),
    ]
    for i, (block, buffer) in enumerate(zip(blocks, buffers)):
        first = pl.multiple_of(owner_of(block, chips) * rows, rows)
        copies.append(pltpu.make_async_copy(x_hbm.at[0, 0, :, :, pl.ds(first, rows)], buffer, sems.at[2 + i]))
    for copy in copies:
        copy.start()
    copies[0].wait()
    for slot in range(slots):
        code = queue[0, slot]
        slot_of[code] = slot
        plan[pl.ds(code, 1), :] = jnp.full((1, plan.shape[1]), slot, jnp.int32)
    live = count[0]

    def order_dy(section):
        for micro in range(half):
            value = raw[slot_of[section * half + micro]]
            dy_ref[section, micro * tokens : (micro + 1) * tokens, :] = jnp.where(
                micro < live, value, jnp.zeros_like(value)
            )

    copies[1].wait()
    order_dy(0)
    copies[2].wait()

    def x_of(slot, start, size):
        return buffers[0][slot, :, start : start + size]

    def store(span, total):
        out[span, :] = total.astype(out.dtype)

    section_product([slot_of[micro] for micro in range(half)], 0, x_of, dy_ref, rows, store)
    order_dy(1)
    for copy in copies[3:]:
        copy.wait()


COSTS = dict()


def cost(name):
    return pl.CostEstimate(flops=COSTS.get(name, 1), bytes_accessed=1, transcendentals=0)


SMEM = pl.BlockSpec(memory_space=pltpu.SMEM)
VMEM = pl.BlockSpec(memory_space=pltpu.VMEM)
HBM = pl.BlockSpec(memory_space=pl.ANY)


def first_product(queue, count, x, dy, chips, blocks):
    slots, tokens, features = x.shape[2:]
    width = dy.shape[4]
    rows = features // (2 * chips)
    return pl.pallas_call(
        functools.partial(first_kernel, chips, blocks),
        out_shape=(
            pltpu.VMEM((rows, width), jnp.bfloat16),
            pltpu.VMEM((slots, 128), jnp.int32),
            pltpu.VMEM((2, slots // 2 * tokens, width), dy.dtype),
        )
        + (pltpu.VMEM((slots, tokens, rows), x.dtype),) * len(blocks),
        in_specs=[HBM, SMEM, HBM, HBM],
        out_specs=(VMEM,) * (3 + len(blocks)),
        scratch_shapes=[
            pltpu.VMEM((slots, tokens, width), dy.dtype),
            pltpu.SMEM(queue.shape, queue.dtype),
            pltpu.SMEM((slots,), jnp.int32),
            pltpu.SemaphoreType.DMA((2 + len(blocks),)),
        ],
        compiler_params=vmem_limit(54),
        cost_estimate=cost("first_product"),
        name="first_product",
    )(queue, count, x, dy)


def product(plan, x, dy, block, section, chips, rows, other=None, stacked=False, beside=None, dtype=jnp.bfloat16, name=""):
    width = dy.shape[2]
    operands = [plan, x, dy] + ([] if other is None else [other]) + ([] if beside is None else [beside])
    shape = (2, rows, width) if stacked else (rows, width)
    return pl.pallas_call(
        functools.partial(product_kernel, section, chips, block, other is not None, section if stacked else None),
        out_shape=jax.ShapeDtypeStruct(shape, dtype),
        in_specs=[VMEM] * len(operands),
        out_specs=VMEM,
        input_output_aliases={} if beside is None else {len(operands) - 1: 0},
        compiler_params=vmem_limit(8),
        cost_estimate=cost(name),
        name=name,
    )(*operands)


def sum_kernel(a, b, out):
    sections, rows, _ = a.shape
    slab = 64
    per = rows // slab

    def step(i, carry):
        section, span = lax.div(i, per), pl.ds(pl.multiple_of(lax.rem(i, per) * slab, slab), slab)
        out[section, span, :] = (
            a[section, span, :].astype(jnp.float32) + b[section, span, :].astype(jnp.float32)
        ).astype(out.dtype)
        return carry

    lax.fori_loop(0, sections * per, step, 0)


def add(a, b):
    return pl.pallas_call(
        sum_kernel,
        out_shape=jax.ShapeDtypeStruct(a.shape, a.dtype),
        in_specs=[VMEM, VMEM],
        out_specs=VMEM,
        compiler_params=vmem_limit(4),
        cost_estimate=cost("ring_add"),
        name="ring_add",
    )(a, b)


def total_kernel(own, summed, plain, grad, squares):
    slab = 32
    _, rows, width = own.shape

    def step(i, kept):
        span = pl.ds(pl.multiple_of(i * slab, slab), slab)
        for section in range(own.shape[0]):
            total = own[section, span, :] + summed[section, span, :].astype(jnp.float32)
            total = total + plain[section, span, :].astype(jnp.float32)
            grad[section, span, :] = total
            kept = kept + total * total
        return kept

    kept = lax.fori_loop(0, rows // slab, step, jnp.zeros((slab, width), jnp.float32))
    squares[...] = jnp.full(squares.shape, jnp.sum(kept), jnp.float32)


def totals(peers, own, summed, plain):
    return pl.pallas_call(
        total_kernel,
        out_shape=(
            jax.ShapeDtypeStruct(own.shape, jnp.float32),
            jax.ShapeDtypeStruct((peers, 128), jnp.float32),
        ),
        in_specs=[VMEM] * 3,
        out_specs=(VMEM, VMEM),
        compiler_params=vmem_limit(4),
        cost_estimate=cost("totals"),
        name="totals",
    )(own, summed, plain)


def update_kernel(max_norm, squares, grad, master, moment, variance, new_master, new_moment, norm_out, masters, moments, sems):
    norm = jnp.sqrt(jnp.sum(squares[:, 0:1]))
    clip = jnp.minimum(jnp.float32(1.0), max_norm / (norm + 1e-06))
    norm_out[0, 0] = norm
    sections, rows, width = grad.shape
    chunk, slab = 128, 64
    per = rows // chunk

    def copies(i):
        section, span = lax.div(i, per), pl.ds(pl.multiple_of(lax.rem(i, per) * chunk, chunk), chunk)
        return (
            pltpu.make_async_copy(masters.at[section, span], new_master.at[section, span], sems.at[0, i]),
            pltpu.make_async_copy(moments.at[section, span], new_moment.at[section, span], sems.at[1, i]),
        )

    def one(i, carry):
        section = lax.div(i, per)

        def step(j, inner):
            span = pl.ds(pl.multiple_of(lax.rem(i, per) * chunk + j * slab, slab), slab)
            scaled = clip * grad[section, span, :]
            fresh = 0.9 * moment[section, span, :] + 0.1 * scaled
            second = (0.95 / second_fix) * variance[section, span, :] + (0.05 / second_fix) * (scaled * scaled)
            update = ((0.01 / first_fix) * fresh) / (second * lax.rsqrt(second) + 1e-08)
            moments[section, span, :] = fresh
            masters[section, span, :] = (1.0 - 0.001) * master[section, span, :] - update
            return inner

        lax.fori_loop(0, chunk // slab, step, 0)
        for copy in copies(i):
            copy.start()
        return carry

    lax.fori_loop(0, sections * per, one, 0)

    def finish(i, carry):
        for copy in copies(i):
            copy.wait()
        return carry

    lax.fori_loop(0, sections * per, finish, 0)


def adam(max_norm, squares, grad, master, moment, variance):
    sections, rows, width = grad.shape
    state = jax.ShapeDtypeStruct(grad.shape, jnp.float32)
    return pl.pallas_call(
        functools.partial(update_kernel, max_norm),
        out_shape=(state, state, jax.ShapeDtypeStruct((1, 1), jnp.float32)),
        in_specs=[VMEM] * 5,
        out_specs=(HBM, HBM, SMEM),
        scratch_shapes=[
            pltpu.VMEM(grad.shape, jnp.float32),
            pltpu.VMEM(grad.shape, jnp.float32),
            pltpu.SemaphoreType.DMA((2, sections * rows // 128)),
        ],
        compiler_params=vmem_limit(8),
        cost_estimate=cost("adam"),
        name="adam",
    )(squares, grad, master, moment, variance)


def after(value, *earlier):
    return lax.optimization_barrier((value, earlier))[0]


def on_device(stash_x, stash_dy, queue, micro_count, master, moment, variance):
    own_rows, kv_width = master.shape[2:]
    peers = lax.axis_size("dp")
    chips = peers // 2
    everyone = lax.axis_size("pipe") * peers
    hbm_queue, hbm_x, hbm_dy = (
        pltpu.with_memory_space_constraint(value, pltpu.HBM) for value in (queue, stash_x, stash_dy)
    )

    held_x = pltpu.with_memory_space_constraint(stash_x, pltpu.VMEM)

    def ring(sign):
        return [
            (i, (i // 2 + sign * (1 - 2 * (i % 2))) % chips * 2 + i % 2) for i in range(peers)
        ]

    def sibling(value):
        return lax.ppermute(value, "dp", [(i, i ^ 1) for i in range(peers)])

    def along(value):
        return lax.ppermute(value, "dp", ring(1))

    def against(value):
        return lax.ppermute(value, "dp", ring(-1))

    sent_a, plan, dy, x_send, x_keep = first_product(hbm_queue, micro_count, hbm_x, hbm_dy, chips, ((-2, False), (2, True)))
    far_other = [sibling(sent_a)]
    block = functools.partial(product, plan, chips=chips, rows=own_rows)
    sent_b = block(x_send, dy, (-2, False), 1, name="far_send_b")
    far_other.append(sibling(sent_b))
    others = {}

    def send(step, dy):
        others[-step] = []
        for section in range(2):
            sent = block(held_x, dy, (step, False), section, name=f"send_{step % chips}{'ab'[section]}")
            others[-step].append(sibling(sent))
            dy = after(dy, sent)
        return dy

    def keep(step, x, other, dy, dtype=jnp.bfloat16):
        kept = None
        for section in range(2):
            kept = block(
                x,
                dy,
                (step, True),
                section,
                other=other[section],
                stacked=True,
                beside=kept,
                dtype=dtype,
                name=f"keep_{step % chips}{'ab'[section]}",
            )
            dy = after(dy, kept)
        return kept

    far = keep(2, x_keep, far_other, after(dy, sent_b))
    came = along(far)
    dy = send(0, after(dy, far))
    dy = send(-1, dy)
    dy = send(1, dy)
    near_a = keep(1, held_x, others[1], dy)
    near_b = keep(-1, held_x, others[-1], after(dy, near_a))
    plain = against(near_b)
    near_a = add(after(near_a, near_b), came)
    summed = along(near_a)
    own = keep(0, held_x, others[0], after(dy, near_a), jnp.float32)
    grad, squares = totals(everyone, own, summed, plain)
    squares = lax.all_to_all(squares, ("pipe", "dp"), 0, 0, tiled=True)
    max_norm = 0.05 * math.sqrt(2 * lax.axis_size("pipe") * own_rows * peers * kv_width)
    new_master, new_moment, norm = adam(max_norm, squares, grad, master[0], moment[0], variance[0])
    return (new_master[None], new_moment[None], norm[0, 0])


def solution(mesh):
    in_specs = (
        P("pipe", "dp", None, None, None),
        P("pipe", "dp", None, None, None),
        P("pipe", None),
        P("dp"),
        P("pipe", None, "dp", None),
        P("pipe", None, "dp", None),
        P("pipe", None, "dp", None),
    )
    out_specs = (P("pipe", None, "dp", None), P("pipe", None, "dp", None), P())
    return jax.shard_map(
        on_device, mesh=mesh, in_specs=in_specs, out_specs=out_specs, check_vma=False
    )
```

```python
import functools
import math

import jax
import jax.numpy as jnp
from jax import lax
from jax.experimental import pallas as pl
from jax.experimental.pallas import tpu as pltpu
from jax.sharding import PartitionSpec as P

first_fix = 1.0 - 0.9**20
second_fix = 1.0 - 0.95**20

def vmem_limit(mib):
    return pltpu.CompilerParams(vmem_limit_bytes=mib * 1024 * 1024)


def place():
    me = lax.axis_index("dp")
    core = lax.rem(me, 2)
    return lax.div(me, 2), core, 1 - 2 * core


def owner_of(block, chips):
    step, mine = block
    z, core, sign = place()
    target = lax.rem(z + chips + step * sign, chips)
    return 2 * target + (core if mine else 1 - core)


def section_product(slots, section, x_of, dy_ref, rows, store):
    tile = min(256, rows)
    for start in range(0, rows, tile):
        x = jnp.concatenate([x_of(slot, start, tile) for slot in slots], axis=0)
        store(
            pl.ds(start, tile),
            lax.dot_general(x, dy_ref[section], (((0,), (0,)), ((), ())), preferred_element_type=jnp.float32),
        )


def product_kernel(section, chips, block, has_other, place_in, *refs):
    plan, x_ref, dy_ref = refs[:3]
    out = refs[-1]
    rows = out.shape[-2]
    half = plan.shape[0] // 2
    slots = [plan[section * half + micro, 0] for micro in range(half)]
    first = owner_of(block, chips) * rows

    def x_of(slot, start, size):
        if len(x_ref.shape) == 3:
            return x_ref[slot, :, start : start + size]
        return x_ref[0, 0, slot, :, pl.ds(pl.multiple_of(first + start, size), size)]

    def store(span, total):
        if has_other:
            total = total + refs[3][span, :].astype(jnp.float32)
        if place_in is None:
            out[span, :] = total.astype(out.dtype)
        else:
            out[place_in, span, :] = total.astype(out.dtype)

    section_product(slots, section, x_of, dy_ref, rows, store)


def first_kernel(chips, blocks, queue_hbm, count, x_hbm, dy_hbm, out, plan, dy_ref, *rest):
    buffers, (raw, queue, slot_of, sems) = rest[:-4], rest[-4:]
    rows = buffers[0].shape[2]
    slots, tokens, _ = raw.shape
    half = slots // 2
    copies = [
        pltpu.make_async_copy(queue_hbm, queue, sems.at[0]),
        pltpu.make_async_copy(dy_hbm.at[0, 0], raw, sems.at[1]),
    ]
    for i, (block, buffer) in enumerate(zip(blocks, buffers)):
        first = pl.multiple_of(owner_of(block, chips) * rows, rows)
        copies.append(pltpu.make_async_copy(x_hbm.at[0, 0, :, :, pl.ds(first, rows)], buffer, sems.at[2 + i]))
    for copy in copies:
        copy.start()
    copies[0].wait()
    for slot in range(slots):
        code = queue[0, slot]
        slot_of[code] = slot
        plan[pl.ds(code, 1), :] = jnp.full((1, plan.shape[1]), slot, jnp.int32)
    live = count[0]

    def order_dy(section):
        for micro in range(half):
            value = raw[slot_of[section * half + micro]]
            dy_ref[section, micro * tokens : (micro + 1) * tokens, :] = jnp.where(
                micro < live, value, jnp.zeros_like(value)
            )

    copies[1].wait()
    order_dy(0)
    copies[2].wait()

    def x_of(slot, start, size):
        return buffers[0][slot, :, start : start + size]

    def store(span, total):
        out[span, :] = total.astype(out.dtype)

    section_product([slot_of[micro] for micro in range(half)], 0, x_of, dy_ref, rows, store)
    order_dy(1)
    for copy in copies[3:]:
        copy.wait()


COSTS = dict()


def cost(name):
    return pl.CostEstimate(flops=COSTS.get(name, 1), bytes_accessed=1, transcendentals=0)


SMEM = pl.BlockSpec(memory_space=pltpu.SMEM)
VMEM = pl.BlockSpec(memory_space=pltpu.VMEM)
HBM = pl.BlockSpec(memory_space=pl.ANY)


def first_product(queue, count, x, dy, chips, blocks):
    slots, tokens, features = x.shape[2:]
    width = dy.shape[4]
    rows = features // (2 * chips)
    return pl.pallas_call(
        functools.partial(first_kernel, chips, blocks),
        out_shape=(
            pltpu.VMEM((rows, width), jnp.bfloat16),
            pltpu.VMEM((slots, 128), jnp.int32),
            pltpu.VMEM((2, slots // 2 * tokens, width), dy.dtype),
        )
        + (pltpu.VMEM((slots, tokens, rows), x.dtype),) * len(blocks),
        in_specs=[HBM, SMEM, HBM, HBM],
        out_specs=(VMEM,) * (3 + len(blocks)),
        scratch_shapes=[
            pltpu.VMEM((slots, tokens, width), dy.dtype),
            pltpu.SMEM(queue.shape, queue.dtype),
            pltpu.SMEM((slots,), jnp.int32),
            pltpu.SemaphoreType.DMA((2 + len(blocks),)),
        ],
        compiler_params=vmem_limit(54),
        cost_estimate=cost("first_product"),
        name="first_product",
    )(queue, count, x, dy)


def product(plan, x, dy, block, section, chips, rows, other=None, stacked=False, beside=None, dtype=jnp.bfloat16, name=""):
    width = dy.shape[2]
    operands = [plan, x, dy] + ([] if other is None else [other]) + ([] if beside is None else [beside])
    shape = (2, rows, width) if stacked else (rows, width)
    return pl.pallas_call(
        functools.partial(product_kernel, section, chips, block, other is not None, section if stacked else None),
        out_shape=jax.ShapeDtypeStruct(shape, dtype),
        in_specs=[VMEM] * len(operands),
        out_specs=VMEM,
        input_output_aliases={} if beside is None else {len(operands) - 1: 0},
        compiler_params=vmem_limit(8),
        cost_estimate=cost(name),
        name=name,
    )(*operands)


def sum_kernel(section, a, b, out):
    sections, rows, _ = a.shape
    slab = 64
    per = rows // slab

    def step(i, carry):
        span = pl.ds(pl.multiple_of(lax.rem(i, per) * slab, slab), slab)
        if section is None:
            place_in = lax.div(i, per)
            other = b[place_in, span, :]
        else:
            place_in = section
            other = b[span, :]
        out[place_in, span, :] = (a[place_in, span, :].astype(jnp.float32) + other.astype(jnp.float32)).astype(out.dtype)
        return carry

    lax.fori_loop(0, per * (sections if section is None else 1), step, 0)


def add(a, b, section=None):
    name = "ring_add" if section is None else f"far_add_{'ab'[section]}"
    return pl.pallas_call(
        functools.partial(sum_kernel, section),
        out_shape=jax.ShapeDtypeStruct(a.shape, a.dtype),
        in_specs=[VMEM, VMEM],
        out_specs=VMEM,
        input_output_aliases={0: 0},
        compiler_params=vmem_limit(4),
        cost_estimate=cost("ring_add"),
        name=name,
    )(a, b)


def total_kernel(own, summed, plain, grad, squares):
    slab = 32
    _, rows, width = own.shape

    def step(i, kept):
        span = pl.ds(pl.multiple_of(i * slab, slab), slab)
        for section in range(own.shape[0]):
            total = own[section, span, :] + summed[section, span, :].astype(jnp.float32)
            total = total + plain[section, span, :].astype(jnp.float32)
            grad[section, span, :] = total
            kept = kept + total * total
        return kept

    kept = lax.fori_loop(0, rows // slab, step, jnp.zeros((slab, width), jnp.float32))
    squares[...] = jnp.full(squares.shape, jnp.sum(kept), jnp.float32)


def totals(peers, own, summed, plain):
    return pl.pallas_call(
        total_kernel,
        out_shape=(
            jax.ShapeDtypeStruct(own.shape, jnp.float32),
            jax.ShapeDtypeStruct((peers, 128), jnp.float32),
        ),
        in_specs=[VMEM] * 3,
        out_specs=(VMEM, VMEM),
        compiler_params=vmem_limit(4),
        cost_estimate=cost("totals"),
        name="totals",
    )(own, summed, plain)


def update_kernel(max_norm, squares, grad, master, moment, variance, new_master, new_moment, norm_out, masters, moments, sems):
    norm = jnp.sqrt(jnp.sum(squares[:, 0:1]))
    clip = jnp.minimum(jnp.float32(1.0), max_norm / (norm + 1e-06))
    norm_out[0, 0] = norm
    sections, rows, width = grad.shape
    chunk, slab = 128, 128
    per = rows // chunk

    def copies(i):
        section, span = lax.div(i, per), pl.ds(pl.multiple_of(lax.rem(i, per) * chunk, chunk), chunk)
        return (
            pltpu.make_async_copy(masters.at[section, span], new_master.at[section, span], sems.at[0, i]),
            pltpu.make_async_copy(moments.at[section, span], new_moment.at[section, span], sems.at[1, i]),
        )

    def one(i, carry):
        section = lax.div(i, per)

        def step(j, inner):
            span = pl.ds(pl.multiple_of(lax.rem(i, per) * chunk + j * slab, slab), slab)
            scaled = clip * grad[section, span, :]
            fresh = 0.9 * moment[section, span, :] + 0.1 * scaled
            second = (0.95 / second_fix) * variance[section, span, :] + (0.05 / second_fix) * (scaled * scaled)
            update = ((0.01 / first_fix) * fresh) / (second * lax.rsqrt(second) + 1e-08)
            moments[section, span, :] = fresh
            masters[section, span, :] = (1.0 - 0.001) * master[section, span, :] - update
            return inner

        lax.fori_loop(0, chunk // slab, step, 0)
        for copy in copies(i):
            copy.start()
        return carry

    lax.fori_loop(0, sections * per, one, 0)

    def finish(i, carry):
        for copy in copies(i):
            copy.wait()
        return carry

    lax.fori_loop(0, sections * per, finish, 0)


def adam(max_norm, squares, grad, master, moment, variance):
    sections, rows, width = grad.shape
    state = jax.ShapeDtypeStruct(grad.shape, jnp.float32)
    return pl.pallas_call(
        functools.partial(update_kernel, max_norm),
        out_shape=(state, state, jax.ShapeDtypeStruct((1, 1), jnp.float32)),
        in_specs=[VMEM] * 5,
        out_specs=(HBM, HBM, SMEM),
        scratch_shapes=[
            pltpu.VMEM(grad.shape, jnp.float32),
            pltpu.VMEM(grad.shape, jnp.float32),
            pltpu.SemaphoreType.DMA((2, sections * rows // 128)),
        ],
        compiler_params=vmem_limit(8),
        cost_estimate=cost("adam"),
        name="adam",
    )(squares, grad, master, moment, variance)


def after(value, *earlier):
    return lax.optimization_barrier((value, earlier))[0]


def on_device(stash_x, stash_dy, queue, micro_count, master, moment, variance):
    own_rows, kv_width = master.shape[2:]
    peers = lax.axis_size("dp")
    chips = peers // 2
    everyone = lax.axis_size("pipe") * peers
    hbm_queue, hbm_x, hbm_dy = (
        pltpu.with_memory_space_constraint(value, pltpu.HBM) for value in (queue, stash_x, stash_dy)
    )

    held_x = pltpu.with_memory_space_constraint(stash_x, pltpu.VMEM)

    def ring(sign):
        return [
            (i, (i // 2 + sign * (1 - 2 * (i % 2))) % chips * 2 + i % 2) for i in range(peers)
        ]

    def sibling(value):
        return lax.ppermute(value, "dp", [(i, i ^ 1) for i in range(peers)])

    def along(value):
        return lax.ppermute(value, "dp", ring(1))

    def against(value):
        return lax.ppermute(value, "dp", ring(-1))

    sent_a, plan, dy, x_send, x_keep = first_product(hbm_queue, micro_count, hbm_x, hbm_dy, chips, ((-2, False), (2, True)))
    far_other = [sibling(sent_a)]
    block = functools.partial(product, plan, chips=chips, rows=own_rows)
    sent_b = block(x_send, dy, (-2, False), 1, name="far_send_b")
    far_other.append(sibling(sent_b))
    others = {}

    def send(step, dy):
        others[-step] = []
        for section in range(2):
            sent = block(held_x, dy, (step, False), section, name=f"send_{step % chips}{'ab'[section]}")
            others[-step].append(sibling(sent))
            dy = after(dy, sent)
        return dy

    def keep(step, x, other, dy, dtype=jnp.bfloat16):
        kept = None
        for section in range(2):
            kept = block(
                x,
                dy,
                (step, True),
                section,
                other=other[section],
                stacked=True,
                beside=kept,
                dtype=dtype,
                name=f"keep_{step % chips}{'ab'[section]}",
            )
            dy = after(dy, kept)
        return kept

    far = block(x_keep, after(dy, sent_b), (2, True), 0, stacked=True, name="keep_2a")
    far = block(x_keep, dy, (2, True), 1, stacked=True, beside=far, name="keep_2b")
    far = add(far, far_other[0], 0)
    far = add(far, far_other[1], 1)
    came = along(far)
    dy = send(0, after(dy, far))
    dy = send(-1, dy)
    dy = send(1, dy)
    near_a = keep(1, held_x, others[1], dy)
    near_b = keep(-1, held_x, others[-1], after(dy, near_a))
    plain = against(near_b)
    near_a = add(after(near_a, near_b), came)
    summed = along(near_a)
    own = keep(0, held_x, others[0], after(dy, near_a), jnp.float32)
    grad, squares = totals(everyone, own, summed, plain)
    squares = lax.all_to_all(squares, ("pipe", "dp"), 0, 0, tiled=True)
    max_norm = 0.05 * math.sqrt(2 * lax.axis_size("pipe") * own_rows * peers * kv_width)
    new_master, new_moment, norm = adam(max_norm, squares, grad, master[0], moment[0], variance[0])
    return (new_master[None], new_moment[None], norm[0, 0])


def solution(mesh):
    in_specs = (
        P("pipe", "dp", None, None, None),
        P("pipe", "dp", None, None, None),
        P("pipe", None),
        P("dp"),
        P("pipe", None, "dp", None),
        P("pipe", None, "dp", None),
        P("pipe", None, "dp", None),
    )
    out_specs = (P("pipe", None, "dp", None), P("pipe", None, "dp", None), P())
    return jax.shard_map(
        on_device, mesh=mesh, in_specs=in_specs, out_specs=out_specs, check_vma=False
    )
```

```python
import functools
import math

import jax
import jax.numpy as jnp
from jax import lax
from jax.experimental import pallas as pl
from jax.experimental.pallas import tpu as pltpu
from jax.sharding import PartitionSpec as P

first_fix = 1.0 - 0.9**20
second_fix = 1.0 - 0.95**20

def vmem_limit(mib):
    return pltpu.CompilerParams(vmem_limit_bytes=mib * 1024 * 1024)


def place():
    me = lax.axis_index("dp")
    core = lax.rem(me, 2)
    return lax.div(me, 2), core, 1 - 2 * core


def owner_of(block, chips):
    step, mine = block
    z, core, sign = place()
    target = lax.rem(z + chips + step * sign, chips)
    return 2 * target + (core if mine else 1 - core)


def section_product(slots, section, x_of, dy_ref, rows, store):
    tile = min(256, rows)
    for start in range(0, rows, tile):
        x = jnp.concatenate([x_of(slot, start, tile) for slot in slots], axis=0)
        store(
            pl.ds(start, tile),
            lax.dot_general(x, dy_ref[section], (((0,), (0,)), ((), ())), preferred_element_type=jnp.float32),
        )


def product_kernel(section, chips, block, n_others, place_in, *refs):
    plan, x_ref, dy_ref = refs[:3]
    out = refs[-1]
    rows = out.shape[-2]
    half = plan.shape[0] // 2
    slots = [plan[section * half + micro, 0] for micro in range(half)]
    first = owner_of(block, chips) * rows

    def x_of(slot, start, size):
        if len(x_ref.shape) == 3:
            return x_ref[slot, :, start : start + size]
        return x_ref[0, 0, slot, :, pl.ds(pl.multiple_of(first + start, size), size)]

    def store(span, total):
        for ref in refs[3 : 3 + n_others]:
            other = ref[span, :] if len(ref.shape) == 2 else ref[section, span, :]
            total = total + other.astype(jnp.float32)
        if place_in is None:
            out[span, :] = total.astype(out.dtype)
        else:
            out[place_in, span, :] = total.astype(out.dtype)

    section_product(slots, section, x_of, dy_ref, rows, store)


def first_kernel(chips, blocks, queue_hbm, count, x_hbm, dy_hbm, out, plan, dy_ref, *rest):
    buffers, (raw, queue, slot_of, sems) = rest[:-4], rest[-4:]
    rows = buffers[0].shape[2]
    slots, tokens, _ = raw.shape
    half = slots // 2
    copies = [
        pltpu.make_async_copy(queue_hbm, queue, sems.at[0]),
        pltpu.make_async_copy(dy_hbm.at[0, 0], raw, sems.at[1]),
    ]
    for i, (block, buffer) in enumerate(zip(blocks, buffers)):
        first = pl.multiple_of(owner_of(block, chips) * rows, rows)
        copies.append(pltpu.make_async_copy(x_hbm.at[0, 0, :, :, pl.ds(first, rows)], buffer, sems.at[2 + i]))
    for copy in copies:
        copy.start()
    copies[0].wait()
    for slot in range(slots):
        code = queue[0, slot]
        slot_of[code] = slot
        plan[pl.ds(code, 1), :] = jnp.full((1, plan.shape[1]), slot, jnp.int32)
    live = count[0]

    def order_dy(section):
        for micro in range(half):
            value = raw[slot_of[section * half + micro]]
            dy_ref[section, micro * tokens : (micro + 1) * tokens, :] = jnp.where(
                micro < live, value, jnp.zeros_like(value)
            )

    copies[1].wait()
    order_dy(0)
    copies[2].wait()

    def x_of(slot, start, size):
        return buffers[0][slot, :, start : start + size]

    def store(span, total):
        out[span, :] = total.astype(out.dtype)

    section_product([slot_of[micro] for micro in range(half)], 0, x_of, dy_ref, rows, store)
    order_dy(1)
    for copy in copies[3:]:
        copy.wait()


COSTS = dict()


def cost(name):
    return pl.CostEstimate(flops=COSTS.get(name, 1), bytes_accessed=1, transcendentals=0)


SMEM = pl.BlockSpec(memory_space=pltpu.SMEM)
VMEM = pl.BlockSpec(memory_space=pltpu.VMEM)
HBM = pl.BlockSpec(memory_space=pl.ANY)


def first_product(queue, count, x, dy, chips, blocks):
    slots, tokens, features = x.shape[2:]
    width = dy.shape[4]
    rows = features // (2 * chips)
    return pl.pallas_call(
        functools.partial(first_kernel, chips, blocks),
        out_shape=(
            pltpu.VMEM((rows, width), jnp.bfloat16),
            pltpu.VMEM((slots, 128), jnp.int32),
            pltpu.VMEM((2, slots // 2 * tokens, width), dy.dtype),
        )
        + (pltpu.VMEM((slots, tokens, rows), x.dtype),) * len(blocks),
        in_specs=[HBM, SMEM, HBM, HBM],
        out_specs=(VMEM,) * (3 + len(blocks)),
        scratch_shapes=[
            pltpu.VMEM((slots, tokens, width), dy.dtype),
            pltpu.SMEM(queue.shape, queue.dtype),
            pltpu.SMEM((slots,), jnp.int32),
            pltpu.SemaphoreType.DMA((2 + len(blocks),)),
        ],
        compiler_params=vmem_limit(54),
        cost_estimate=cost("first_product"),
        name="first_product",
    )(queue, count, x, dy)


def product(plan, x, dy, block, section, chips, rows, others=(), stacked=False, beside=None, dtype=jnp.bfloat16, name=""):
    width = dy.shape[2]
    operands = [plan, x, dy, *others] + ([] if beside is None else [beside])
    shape = (2, rows, width) if stacked else (rows, width)
    return pl.pallas_call(
        functools.partial(product_kernel, section, chips, block, len(others), section if stacked else None),
        out_shape=jax.ShapeDtypeStruct(shape, dtype),
        in_specs=[VMEM] * len(operands),
        out_specs=VMEM,
        input_output_aliases={} if beside is None else {len(operands) - 1: 0},
        compiler_params=vmem_limit(8),
        cost_estimate=cost(name),
        name=name,
    )(*operands)


def sum_kernel(section, a, b, out):
    sections, rows, _ = a.shape
    slab = 64
    per = rows // slab

    def step(i, carry):
        span = pl.ds(pl.multiple_of(lax.rem(i, per) * slab, slab), slab)
        if section is None:
            place_in = lax.div(i, per)
            other = b[place_in, span, :]
        else:
            place_in = section
            other = b[span, :]
        out[place_in, span, :] = (a[place_in, span, :].astype(jnp.float32) + other.astype(jnp.float32)).astype(out.dtype)
        return carry

    lax.fori_loop(0, per * (sections if section is None else 1), step, 0)


def add(a, b, section=None):
    name = "ring_add" if section is None else f"far_add_{'ab'[section]}"
    return pl.pallas_call(
        functools.partial(sum_kernel, section),
        out_shape=jax.ShapeDtypeStruct(a.shape, a.dtype),
        in_specs=[VMEM, VMEM],
        out_specs=VMEM,
        input_output_aliases={0: 0},
        compiler_params=vmem_limit(4),
        cost_estimate=cost("ring_add"),
        name=name,
    )(a, b)


def total_kernel(own, summed, grad, squares):
    slab = 32
    _, rows, width = own.shape

    def step(i, kept):
        span = pl.ds(pl.multiple_of(i * slab, slab), slab)
        for section in range(own.shape[0]):
            total = own[section, span, :] + summed[section, span, :].astype(jnp.float32)
            grad[section, span, :] = total
            kept = kept + total * total
        return kept

    kept = lax.fori_loop(0, rows // slab, step, jnp.zeros((slab, width), jnp.float32))
    squares[...] = jnp.full(squares.shape, jnp.sum(kept), jnp.float32)


def totals(peers, own, summed):
    return pl.pallas_call(
        total_kernel,
        out_shape=(
            jax.ShapeDtypeStruct(own.shape, jnp.float32),
            jax.ShapeDtypeStruct((peers, 128), jnp.float32),
        ),
        in_specs=[VMEM] * 2,
        out_specs=(VMEM, VMEM),
        compiler_params=vmem_limit(4),
        cost_estimate=cost("totals"),
        name="totals",
    )(own, summed)


def update_kernel(max_norm, squares, grad, master, moment, variance, new_master, new_moment, norm_out, masters, moments, sems):
    norm = jnp.sqrt(jnp.sum(squares[:, 0:1]))
    clip = jnp.minimum(jnp.float32(1.0), max_norm / (norm + 1e-06))
    norm_out[0, 0] = norm
    sections, rows, width = grad.shape
    chunk, slab = 128, 128
    per = rows // chunk

    def copies(i):
        section, span = lax.div(i, per), pl.ds(pl.multiple_of(lax.rem(i, per) * chunk, chunk), chunk)
        return (
            pltpu.make_async_copy(masters.at[section, span], new_master.at[section, span], sems.at[0, i]),
            pltpu.make_async_copy(moments.at[section, span], new_moment.at[section, span], sems.at[1, i]),
        )

    def one(i, carry):
        section = lax.div(i, per)

        def step(j, inner):
            span = pl.ds(pl.multiple_of(lax.rem(i, per) * chunk + j * slab, slab), slab)
            scaled = clip * grad[section, span, :]
            fresh = 0.9 * moment[section, span, :] + 0.1 * scaled
            second = (0.95 / second_fix) * variance[section, span, :] + (0.05 / second_fix) * (scaled * scaled)
            update = ((0.01 / first_fix) * fresh) / (second * lax.rsqrt(second) + 1e-08)
            moments[section, span, :] = fresh
            masters[section, span, :] = (1.0 - 0.001) * master[section, span, :] - update
            return inner

        lax.fori_loop(0, chunk // slab, step, 0)
        for copy in copies(i):
            copy.start()
        return carry

    lax.fori_loop(0, sections * per, one, 0)

    def finish(i, carry):
        for copy in copies(i):
            copy.wait()
        return carry

    lax.fori_loop(0, sections * per, finish, 0)


def adam(max_norm, squares, grad, master, moment, variance):
    sections, rows, width = grad.shape
    state = jax.ShapeDtypeStruct(grad.shape, jnp.float32)
    return pl.pallas_call(
        functools.partial(update_kernel, max_norm),
        out_shape=(state, state, jax.ShapeDtypeStruct((1, 1), jnp.float32)),
        in_specs=[VMEM] * 5,
        out_specs=(HBM, HBM, SMEM),
        scratch_shapes=[
            pltpu.VMEM(grad.shape, jnp.float32),
            pltpu.VMEM(grad.shape, jnp.float32),
            pltpu.SemaphoreType.DMA((2, sections * rows // 128)),
        ],
        compiler_params=vmem_limit(8),
        cost_estimate=cost("adam"),
        name="adam",
    )(squares, grad, master, moment, variance)


def after(value, *earlier):
    return lax.optimization_barrier((value, earlier))[0]


def on_device(stash_x, stash_dy, queue, micro_count, master, moment, variance):
    own_rows, kv_width = master.shape[2:]
    peers = lax.axis_size("dp")
    chips = peers // 2
    everyone = lax.axis_size("pipe") * peers
    hbm_queue, hbm_x, hbm_dy = (
        pltpu.with_memory_space_constraint(value, pltpu.HBM) for value in (queue, stash_x, stash_dy)
    )

    held_x = pltpu.with_memory_space_constraint(stash_x, pltpu.VMEM)

    def ring(sign):
        return [
            (i, (i // 2 + sign * (1 - 2 * (i % 2))) % chips * 2 + i % 2) for i in range(peers)
        ]

    def sibling(value):
        return lax.ppermute(value, "dp", [(i, i ^ 1) for i in range(peers)])

    def along(value):
        return lax.ppermute(value, "dp", ring(1))

    def against(value):
        return lax.ppermute(value, "dp", ring(-1))

    sent_a, plan, dy, x_send, x_keep = first_product(hbm_queue, micro_count, hbm_x, hbm_dy, chips, ((-2, False), (2, True)))
    far_other = [sibling(sent_a)]
    block = functools.partial(product, plan, chips=chips, rows=own_rows)
    sent_b = block(x_send, dy, (-2, False), 1, name="far_send_b")
    far_other.append(sibling(sent_b))
    others = {}

    def send(step, dy):
        others[-step] = []
        for section in range(2):
            sent = block(held_x, dy, (step, False), section, name=f"send_{step % chips}{'ab'[section]}")
            others[-step].append(sibling(sent))
            dy = after(dy, sent)
        return dy

    def keep(step, x, other, dy, dtype=jnp.bfloat16, more=()):
        kept = None
        for section in range(2):
            kept = block(
                x,
                dy,
                (step, True),
                section,
                others=(other[section], *more),
                stacked=True,
                beside=kept,
                dtype=dtype,
                name=f"keep_{step % chips}{'ab'[section]}",
            )
            dy = after(dy, kept)
        return kept

    far = block(x_keep, after(dy, sent_b), (2, True), 0, stacked=True, name="keep_2a")
    far = block(x_keep, dy, (2, True), 1, stacked=True, beside=far, name="keep_2b")
    far = add(far, far_other[0], 0)
    far = add(far, far_other[1], 1)
    came = along(far)
    dy = send(0, after(dy, far))
    dy = send(-1, dy)
    dy = send(1, dy)
    near_a = keep(1, held_x, others[1], dy)
    near_b = keep(-1, held_x, others[-1], after(dy, near_a))
    plain = against(near_b)
    near_a = add(after(near_a, near_b), came)
    summed = along(near_a)
    own = keep(0, held_x, others[0], after(dy, near_a), jnp.float32, (plain,))
    grad, squares = totals(everyone, own, summed)
    squares = lax.all_to_all(squares, ("pipe", "dp"), 0, 0, tiled=True)
    max_norm = 0.05 * math.sqrt(2 * lax.axis_size("pipe") * own_rows * peers * kv_width)
    new_master, new_moment, norm = adam(max_norm, squares, grad, master[0], moment[0], variance[0])
    return (new_master[None], new_moment[None], norm[0, 0])


def solution(mesh):
    in_specs = (
        P("pipe", "dp", None, None, None),
        P("pipe", "dp", None, None, None),
        P("pipe", None),
        P("dp"),
        P("pipe", None, "dp", None),
        P("pipe", None, "dp", None),
        P("pipe", None, "dp", None),
    )
    out_specs = (P("pipe", None, "dp", None), P("pipe", None, "dp", None), P())
    return jax.shard_map(
        on_device, mesh=mesh, in_specs=in_specs, out_specs=out_specs, check_vma=False
    )
```

```python
import functools
import math

import jax
import jax.numpy as jnp
from jax import lax
from jax.experimental import pallas as pl
from jax.experimental.pallas import tpu as pltpu
from jax.sharding import PartitionSpec as P

first_fix = 1.0 - 0.9**20
second_fix = 1.0 - 0.95**20

def vmem_limit(mib):
    return pltpu.CompilerParams(vmem_limit_bytes=mib * 1024 * 1024)


def place():
    me = lax.axis_index("dp")
    core = lax.rem(me, 2)
    return lax.div(me, 2), core, 1 - 2 * core


def owner_of(block, chips):
    step, mine = block
    z, core, sign = place()
    target = lax.rem(z + chips + step * sign, chips)
    return 2 * target + (core if mine else 1 - core)


def section_product(slots, section, x_of, dy_ref, rows, store):
    tile = min(256, rows)
    for start in range(0, rows, tile):
        x = jnp.concatenate([x_of(slot, start, tile) for slot in slots], axis=0)
        store(
            pl.ds(start, tile),
            lax.dot_general(x, dy_ref[section], (((0,), (0,)), ((), ())), preferred_element_type=jnp.float32),
        )


def product_kernel(section, chips, block, n_others, place_in, *refs):
    plan, x_ref, dy_ref = refs[:3]
    out = refs[-1]
    rows = out.shape[-2]
    half = plan.shape[0] // 2
    slots = [plan[section * half + micro, 0] for micro in range(half)]
    first = owner_of(block, chips) * rows

    def x_of(slot, start, size):
        if len(x_ref.shape) == 3:
            return x_ref[slot, :, start : start + size]
        return x_ref[0, 0, slot, :, pl.ds(pl.multiple_of(first + start, size), size)]

    def store(span, total):
        for ref in refs[3 : 3 + n_others]:
            other = ref[span, :] if len(ref.shape) == 2 else ref[section, span, :]
            total = total + other.astype(jnp.float32)
        if place_in is None:
            out[span, :] = total.astype(out.dtype)
        else:
            out[place_in, span, :] = total.astype(out.dtype)

    section_product(slots, section, x_of, dy_ref, rows, store)


def first_kernel(chips, blocks, queue_hbm, count, x_hbm, dy_hbm, out, plan, dy_ref, *rest):
    buffers, (raw, queue, slot_of, sems) = rest[:-4], rest[-4:]
    rows = buffers[0].shape[2]
    slots, tokens, _ = raw.shape
    half = slots // 2
    copies = [
        pltpu.make_async_copy(queue_hbm, queue, sems.at[0]),
        pltpu.make_async_copy(dy_hbm.at[0, 0], raw, sems.at[1]),
    ]
    for i, (block, buffer) in enumerate(zip(blocks, buffers)):
        first = pl.multiple_of(owner_of(block, chips) * rows, rows)
        copies.append(pltpu.make_async_copy(x_hbm.at[0, 0, :, :, pl.ds(first, rows)], buffer, sems.at[2 + i]))
    for copy in copies:
        copy.start()
    copies[0].wait()
    for slot in range(slots):
        code = queue[0, slot]
        slot_of[code] = slot
        plan[pl.ds(code, 1), :] = jnp.full((1, plan.shape[1]), slot, jnp.int32)
    live = count[0]

    def order_dy(section):
        for micro in range(half):
            value = raw[slot_of[section * half + micro]]
            dy_ref[section, micro * tokens : (micro + 1) * tokens, :] = jnp.where(
                micro < live, value, jnp.zeros_like(value)
            )

    copies[1].wait()
    order_dy(0)
    copies[2].wait()

    def x_of(slot, start, size):
        return buffers[0][slot, :, start : start + size]

    def store(span, total):
        out[span, :] = total.astype(out.dtype)

    section_product([slot_of[micro] for micro in range(half)], 0, x_of, dy_ref, rows, store)
    order_dy(1)
    for copy in copies[3:]:
        copy.wait()


COSTS = dict()


def cost(name):
    return pl.CostEstimate(flops=COSTS.get(name, 1), bytes_accessed=1, transcendentals=0)


SMEM = pl.BlockSpec(memory_space=pltpu.SMEM)
VMEM = pl.BlockSpec(memory_space=pltpu.VMEM)
HBM = pl.BlockSpec(memory_space=pl.ANY)


def first_product(queue, count, x, dy, chips, blocks):
    slots, tokens, features = x.shape[2:]
    width = dy.shape[4]
    rows = features // (2 * chips)
    return pl.pallas_call(
        functools.partial(first_kernel, chips, blocks),
        out_shape=(
            pltpu.VMEM((rows, width), jnp.bfloat16),
            pltpu.VMEM((slots, 128), jnp.int32),
            pltpu.VMEM((2, slots // 2 * tokens, width), dy.dtype),
        )
        + (pltpu.VMEM((slots, tokens, rows), x.dtype),) * len(blocks),
        in_specs=[HBM, SMEM, HBM, HBM],
        out_specs=(VMEM,) * (3 + len(blocks)),
        scratch_shapes=[
            pltpu.VMEM((slots, tokens, width), dy.dtype),
            pltpu.SMEM(queue.shape, queue.dtype),
            pltpu.SMEM((slots,), jnp.int32),
            pltpu.SemaphoreType.DMA((2 + len(blocks),)),
        ],
        compiler_params=vmem_limit(54),
        cost_estimate=cost("first_product"),
        name="first_product",
    )(queue, count, x, dy)


def product(plan, x, dy, block, section, chips, rows, others=(), stacked=False, beside=None, dtype=jnp.bfloat16, name=""):
    width = dy.shape[2]
    operands = [plan, x, dy, *others] + ([] if beside is None else [beside])
    shape = (2, rows, width) if stacked else (rows, width)
    return pl.pallas_call(
        functools.partial(product_kernel, section, chips, block, len(others), section if stacked else None),
        out_shape=jax.ShapeDtypeStruct(shape, dtype),
        in_specs=[VMEM] * len(operands),
        out_specs=VMEM,
        input_output_aliases={} if beside is None else {len(operands) - 1: 0},
        compiler_params=vmem_limit(8),
        cost_estimate=cost(name),
        name=name,
    )(*operands)


def sum_kernel(section, a, b, out):
    sections, rows, _ = a.shape
    slab = 64
    per = rows // slab

    def step(i, carry):
        span = pl.ds(pl.multiple_of(lax.rem(i, per) * slab, slab), slab)
        if section is None:
            place_in = lax.div(i, per)
            other = b[place_in, span, :]
        else:
            place_in = section
            other = b[span, :]
        out[place_in, span, :] = (a[place_in, span, :].astype(jnp.float32) + other.astype(jnp.float32)).astype(out.dtype)
        return carry

    lax.fori_loop(0, per * (sections if section is None else 1), step, 0)


def add(a, b, section=None):
    name = "ring_add" if section is None else f"far_add_{'ab'[section]}"
    return pl.pallas_call(
        functools.partial(sum_kernel, section),
        out_shape=jax.ShapeDtypeStruct(a.shape, a.dtype),
        in_specs=[VMEM, VMEM],
        out_specs=VMEM,
        input_output_aliases={0: 0},
        compiler_params=vmem_limit(4),
        cost_estimate=cost("ring_add"),
        name=name,
    )(a, b)


def total_kernel(own, summed, grad, squares):
    slab = 64
    _, rows, width = own.shape

    def step(i, kept):
        span = pl.ds(pl.multiple_of(i * slab, slab), slab)
        for section in range(own.shape[0]):
            total = own[section, span, :] + summed[section, span, :].astype(jnp.float32)
            grad[section, span, :] = total
            kept = kept + total * total
        return kept

    kept = lax.fori_loop(0, rows // slab, step, jnp.zeros((slab, width), jnp.float32))
    squares[...] = jnp.full(squares.shape, jnp.sum(kept), jnp.float32)


def totals(peers, own, summed):
    return pl.pallas_call(
        total_kernel,
        out_shape=(
            jax.ShapeDtypeStruct(own.shape, jnp.float32),
            jax.ShapeDtypeStruct((peers, 128), jnp.float32),
        ),
        in_specs=[VMEM] * 2,
        out_specs=(VMEM, VMEM),
        compiler_params=vmem_limit(4),
        cost_estimate=cost("totals"),
        name="totals",
    )(own, summed)


def update_kernel(max_norm, squares, grad, master, moment, variance, new_master, new_moment, norm_out, masters, moments, sems):
    norm = jnp.sqrt(jnp.sum(squares[:, 0:1]))
    clip = jnp.minimum(jnp.float32(1.0), max_norm / (norm + 1e-06))
    norm_out[0, 0] = norm
    sections, rows, width = grad.shape
    chunk, slab = 128, 128
    per = rows // chunk

    def copies(i):
        section, span = lax.div(i, per), pl.ds(pl.multiple_of(lax.rem(i, per) * chunk, chunk), chunk)
        return (
            pltpu.make_async_copy(masters.at[section, span], new_master.at[section, span], sems.at[0, i]),
            pltpu.make_async_copy(moments.at[section, span], new_moment.at[section, span], sems.at[1, i]),
        )

    def one(i, carry):
        section = lax.div(i, per)

        def step(j, inner):
            span = pl.ds(pl.multiple_of(lax.rem(i, per) * chunk + j * slab, slab), slab)
            scaled = clip * grad[section, span, :]
            fresh = 0.9 * moment[section, span, :] + 0.1 * scaled
            second = (0.95 / second_fix) * variance[section, span, :] + (0.05 / second_fix) * (scaled * scaled)
            update = ((0.01 / first_fix) * fresh) / (second * lax.rsqrt(second) + 1e-08)
            moments[section, span, :] = fresh
            masters[section, span, :] = (1.0 - 0.001) * master[section, span, :] - update
            return inner

        lax.fori_loop(0, chunk // slab, step, 0)
        for copy in copies(i):
            copy.start()
        return carry

    lax.fori_loop(0, sections * per, one, 0)

    def finish(i, carry):
        for copy in copies(i):
            copy.wait()
        return carry

    lax.fori_loop(0, sections * per, finish, 0)


def adam(max_norm, squares, grad, master, moment, variance):
    sections, rows, width = grad.shape
    state = jax.ShapeDtypeStruct(grad.shape, jnp.float32)
    return pl.pallas_call(
        functools.partial(update_kernel, max_norm),
        out_shape=(state, state, jax.ShapeDtypeStruct((1, 1), jnp.float32)),
        in_specs=[VMEM] * 5,
        out_specs=(HBM, HBM, SMEM),
        scratch_shapes=[
            pltpu.VMEM(grad.shape, jnp.float32),
            pltpu.VMEM(grad.shape, jnp.float32),
            pltpu.SemaphoreType.DMA((2, sections * rows // 128)),
        ],
        compiler_params=vmem_limit(8),
        cost_estimate=cost("adam"),
        name="adam",
    )(squares, grad, master, moment, variance)


def after(value, *earlier):
    return lax.optimization_barrier((value, earlier))[0]


def on_device(stash_x, stash_dy, queue, micro_count, master, moment, variance):
    own_rows, kv_width = master.shape[2:]
    peers = lax.axis_size("dp")
    chips = peers // 2
    everyone = lax.axis_size("pipe") * peers
    hbm_queue, hbm_x, hbm_dy = (
        pltpu.with_memory_space_constraint(value, pltpu.HBM) for value in (queue, stash_x, stash_dy)
    )

    held_x = pltpu.with_memory_space_constraint(stash_x, pltpu.VMEM)

    def ring(sign):
        return [
            (i, (i // 2 + sign * (1 - 2 * (i % 2))) % chips * 2 + i % 2) for i in range(peers)
        ]

    def sibling(value):
        return lax.ppermute(value, "dp", [(i, i ^ 1) for i in range(peers)])

    def along(value):
        return lax.ppermute(value, "dp", ring(1))

    def against(value):
        return lax.ppermute(value, "dp", ring(-1))

    sent_a, plan, dy, x_send, x_keep = first_product(hbm_queue, micro_count, hbm_x, hbm_dy, chips, ((-2, False), (2, True)))
    far_other = [sibling(sent_a)]
    block = functools.partial(product, plan, chips=chips, rows=own_rows)
    sent_b = block(x_send, dy, (-2, False), 1, name="far_send_b")
    far_other.append(sibling(sent_b))
    others = {}

    def send(step, dy):
        others[-step] = []
        for section in range(2):
            sent = block(held_x, dy, (step, False), section, name=f"send_{step % chips}{'ab'[section]}")
            others[-step].append(sibling(sent))
            dy = after(dy, sent)
        return dy

    def keep(step, x, other, dy, dtype=jnp.bfloat16, more=()):
        kept = None
        for section in range(2):
            kept = block(
                x,
                dy,
                (step, True),
                section,
                others=(other[section], *more),
                stacked=True,
                beside=kept,
                dtype=dtype,
                name=f"keep_{step % chips}{'ab'[section]}",
            )
            dy = after(dy, kept)
        return kept

    far = block(x_keep, after(dy, sent_b), (2, True), 0, stacked=True, name="keep_2a")
    far = block(x_keep, dy, (2, True), 1, stacked=True, beside=far, name="keep_2b")
    far = add(far, far_other[0], 0)
    far = add(far, far_other[1], 1)
    came = along(far)
    dy = send(0, after(dy, far))
    dy = send(-1, dy)
    dy = send(1, dy)
    near_a = keep(1, held_x, others[1], dy)
    near_b = keep(-1, held_x, others[-1], after(dy, near_a))
    plain = against(near_b)
    near_a = add(after(near_a, near_b), came)
    summed = along(near_a)
    own = keep(0, held_x, others[0], after(dy, near_a), jnp.float32, (plain,))
    grad, squares = totals(everyone, own, summed)
    squares = lax.all_to_all(squares, ("pipe", "dp"), 0, 0, tiled=True)
    max_norm = 0.05 * math.sqrt(2 * lax.axis_size("pipe") * own_rows * peers * kv_width)
    new_master, new_moment, norm = adam(max_norm, squares, grad, master[0], moment[0], variance[0])
    return (new_master[None], new_moment[None], norm[0, 0])


def solution(mesh):
    in_specs = (
        P("pipe", "dp", None, None, None),
        P("pipe", "dp", None, None, None),
        P("pipe", None),
        P("dp"),
        P("pipe", None, "dp", None),
        P("pipe", None, "dp", None),
        P("pipe", None, "dp", None),
    )
    out_specs = (P("pipe", None, "dp", None), P("pipe", None, "dp", None), P())
    return jax.shard_map(
        on_device, mesh=mesh, in_specs=in_specs, out_specs=out_specs, check_vma=False
    )
```
